32 devices in a mesh: pairs: 8 (over z, x), ints: 4 (over y, core).
Axes of the slice: x: 2, y: 2, z: 4, core: 2. Of those that a mesh axis runs over, the one named last changes fastest.
Arguments:
- amps: float32 [16, 256, 256], P('pairs', 'ints'), may hold values from -0.8 to 0.8
- resid_rest: float32 [16, 256, 256], P('pairs', 'ints'), may hold values from -6 to 6
- int_blocks: bfloat16 [8, 256, 256], P('pairs'), may hold values from -0.375 to 0.375
- virt_energy: float32 [16, 256], P('pairs'), may hold values from 0.5 to 3
- pair_energy: float32 [16], P('pairs'), may hold values from -2 to -0.5
- item_block: int32 [2048, 1], P(('pairs', 'ints')), may hold values from 0 to 7; in each aligned block of 64 rows (0 to 63, 64 to 127, ...) at most 12 rows name the same one
- share_owner: int32 [768, 1], P('pairs'), may hold values from 0 to 7; in each aligned block of 96 rows (0 to 95, 96 to 191, ...) at most 18 rows name the same one
- share_pair: int32 [768, 1], P('pairs'), may hold values from 0 to 1
- share_amp: int32 [768, 1], P('pairs'), may hold values from 0 to 1
- transpose_pair: int32 [16], P('pairs'), may hold values from 0 to 15, as said below
Outputs:
- update: float32 [16, 256, 256], P('pairs', 'ints')
The draws below stay inside these ranges and needn't reach their ends.
Inputs may be any that keep to these rules, and one draw needn't show every extreme that they name: `item_block`: within each aligned block of 64 rows no value occurs more than 12 times, and some value occurs exactly 12 times. `share_owner`: within each aligned block of 96 rows no value occurs more than 18 times, and some value occurs exactly 18 times. `transpose_pair`: A permutation equal to its own inverse; pair p maps into the block of 2 consecutive pairs whose block number is (p // 2 + 16 // 4) modulo 16 // 2.
All inputs are finite; a program needn't handle non-finite values.
Results may differ from the reference program's by a relative error of at most 0.008.
Values may be sent and summed in bfloat16 or wider, within the bound.
No kernel may reach another device: no remote copies, remote signals or barrier semaphores. Data moves between devices by JAX's collectives and lax.ppermute only.
A program may use at most 64 MiB of HBM per device.

```python
import math
import jax
import jax.numpy as jnp
import numpy as np
from jax import lax

V = 256
PAIR_DEV = 2
RB = 2
NSH = 48
PAIRS = 16
BLOCKS = 8
ITEMS_DEV = 64
ITEMS = 2048
CAP_ITEMS = 12
REQ_DEV = 96
REQS = 768
CAP_SHARE = 18
N_PAIRS = 8
N_INTS = 4


def draw_transpose_pair(key, part):
    half = PAIRS // (2 * PAIR_DEV)
    keys = jax.random.split(jax.random.fold_in(key, 7), half)
    perms = jax.vmap(lambda k: jax.random.permutation(k, PAIR_DEV))(keys).astype(jnp.int32)
    lower = (jnp.arange(half, dtype=jnp.int32)[:, None] + half) * PAIR_DEV + perms
    inverse = jnp.argsort(perms, axis=1).astype(jnp.int32)
    upper = jnp.arange(half, dtype=jnp.int32)[:, None] * PAIR_DEV + inverse
    return jnp.concatenate([lower.reshape(-1), upper.reshape(-1)])


def with_ends(drawn, own_key, low, high):
    spot = [jax.random.randint(jax.random.fold_in(own_key, axis), (), 0, length) for axis, length in enumerate(drawn.shape)]
    main_axis = drawn.shape.index(max(drawn.shape))
    beside = spot[:main_axis] + [(spot[main_axis] + 1) % drawn.shape[main_axis]] + spot[main_axis + 1:]
    return drawn.at[tuple(spot)].set(low).at[tuple(beside)].set(high)


def level_of(rng, extent, cuts, smallest, largest):
    gain = 1.0
    for position, blocks in cuts:
        steps = jax.random.uniform(jax.random.fold_in(jax.random.fold_in(rng, 6), position), (blocks,), jnp.float32, smallest / len(cuts), largest / len(cuts))
        gain = gain * jnp.repeat(jnp.exp(steps), extent[position] // blocks).reshape((-1,) + (1,) * (len(extent) - 1 - position))
    return gain


def routed_block(stream_key, own, number, rows, count, top, reach, lean):
    order = jax.random.permutation(stream_key, count)
    crowded, common = portions_of(count, rows * top, reach, lean, True), portions_of(count, rows * top, reach, lean, False)
    places = jnp.arange(count)

    def named(sizes, offset_by):
        used = int((sizes > 0).sum())
        fixed = max(1, used // 4)
        shifted = fixed + (places - fixed + offset_by * (used - fixed)) % max(1, count - fixed)
        return jnp.zeros((count,), jnp.int32).at[order[jnp.where(places < fixed, places, shifted)]].set(jnp.asarray(sizes, jnp.int32))

    sizes = jnp.where(number % 4 == 0, named(crowded, number // 4), named(common, number - number // 4 - 1))
    mixed = jax.random.permutation(jax.random.fold_in(own, 3), count)
    giver, sink = mixed[0:count // 2 * 2:2], mixed[1:count // 2 * 2:2]
    slack = jnp.minimum(sizes[giver] - 1, reach - sizes[sink]) // 2
    slack = jnp.where((giver == order[0]) | (sink == order[0]) | (sizes[sink] == 0), 0, jnp.maximum(slack, 0))
    shifted = jax.random.randint(jax.random.fold_in(own, 4), (count // 2,), 0, 1 << 20) % (slack + 1)
    sizes = sizes.at[giver].add(-shifted).at[sink].add(shifted)
    labels = jnp.searchsorted(jnp.cumsum(sizes), jnp.arange(rows * top), side="right").astype(jnp.int32)
    listing = labels.reshape(top, rows).T
    listing = listing[jax.random.permutation(jax.random.fold_in(own, 1), rows)]
    offset_by = jax.random.randint(jax.random.fold_in(own, 2), (rows, 1), 0, top)
    return jnp.take_along_axis(listing, (jnp.arange(top)[None, :] + offset_by) % top, axis=1)


def portions_of(amount, total, limit, lean, full):
    loads = [(1 << 20) // math.isqrt(standing ** lean) + 1 for standing in range(1, amount + 1)]
    largest = limit if full else min(limit, max(-(-total // amount), total * loads[0] // sum(loads)))
    least = 1 if total - largest >= amount - 1 else 0
    given, surplus = [largest] + [least] * (amount - 1), total - largest - least * (amount - 1)
    while surplus > 0:
        free = [i for i in range(1, amount) if given[i] < largest] or [i for i in range(1, amount) if given[i] < limit]
        whole, remaining = sum([loads[i] for i in free]), surplus
        for i in free:
            more = min(limit - given[i], max(1, remaining * loads[i] // whole), surplus)
            given[i] = given[i] + more
            surplus = surplus - more
    return np.array(given)


def bell_draw(stream_key, shape, spread, reach, cuts=(), kind=jnp.bfloat16):
    level = level_of(stream_key, shape, cuts, -0.22, 0.18) if cuts else 1.0
    drawn = jax.random.normal(stream_key, shape, jnp.float32) * spread * level
    return jnp.minimum(jnp.maximum(drawn, -reach), reach).astype(kind)


def setup_inputs(seed: int = 0) -> dict:
    splits = jax.random.split(jax.random.key(seed), 11)
    amps = bell_draw(splits[0], (PAIRS, V, V), 0.1, 0.8, ((0, 8), (1, 4)), jnp.float32)
    resid_rest = bell_draw(splits[1], (PAIRS, V, V), 1.0, 6.0, ((0, 8), (1, 4)), jnp.float32)
    int_blocks = bell_draw(splits[2], (BLOCKS, V, V), V ** -0.5, 0.375, ((0, 8),))
    virt_energy = jnp.clip(0.5 + 2.5 * jax.random.uniform(splits[3], (PAIRS, V), jnp.float32) ** level_of(splits[3], (PAIRS, V), ((0, 8),), -0.2, 0.2), 0.5, 3.0)
    pair_energy = jnp.clip(-2.0 + 1.5 * jax.random.uniform(splits[4], (PAIRS,), jnp.float32) ** level_of(splits[4], (PAIRS,), ((0, 8),), -0.2, 0.2), -2.0, -0.5)
    item_block_keys = jax.random.split(jax.random.fold_in(splits[5], 1), ITEMS // ITEMS_DEV)
    item_block_turns = jax.random.permutation(jax.random.fold_in(splits[5], 3), ITEMS // ITEMS_DEV)
    item_block = jax.vmap(lambda own, number: routed_block(jax.random.fold_in(splits[5], 2), own, number, ITEMS_DEV, N_PAIRS, 1, CAP_ITEMS, 2))(item_block_keys, item_block_turns).reshape((ITEMS, 1))
    share_owner_keys = jax.random.split(jax.random.fold_in(splits[6], 1), REQS // REQ_DEV)
    share_owner_turns = jax.random.permutation(jax.random.fold_in(splits[6], 3), REQS // REQ_DEV)
    share_owner = jax.vmap(lambda own, number: routed_block(jax.random.fold_in(splits[6], 2), own, number, REQ_DEV, N_PAIRS, 1, CAP_SHARE, 2))(share_owner_keys, share_owner_turns).reshape((REQS, 1))
    share_pair = with_ends(jax.random.randint(splits[7], (REQS, 1), 0, PAIR_DEV), jax.random.fold_in(splits[7], 1), 0, PAIR_DEV - 1).astype(jnp.int32)
    share_amp = with_ends(jax.random.randint(splits[8], (REQS, 1), 0, PAIR_DEV), jax.random.fold_in(splits[8], 1), 0, PAIR_DEV - 1).astype(jnp.int32)
    transpose_pair = draw_transpose_pair(jax.random.fold_in(splits[10], 71), 0)
    return dict(amps=amps, resid_rest=resid_rest, int_blocks=int_blocks, virt_energy=virt_energy, pair_energy=pair_energy, item_block=item_block, share_owner=share_owner, share_pair=share_pair, share_amp=share_amp, transpose_pair=transpose_pair)


def reference(amps, resid_rest, int_blocks, virt_energy, pair_energy, item_block, share_owner, share_pair, share_amp, transpose_pair):
    amp_half = amps.astype(jnp.bfloat16)
    row_blocks = V // RB
    sub_count = row_blocks // N_INTS
    block_ids = item_block[:, 0].reshape(N_PAIRS, N_INTS, PAIR_DEV, sub_count)
    block_ids = jnp.transpose(block_ids, (0, 2, 1, 3)).reshape(PAIRS, row_blocks)
    row_share = V // N_INTS

    def pair_terms(packed):
        amp_one, ids = packed
        pieces = amp_one.reshape(row_blocks, RB, V).astype(jnp.float32)
        chosen = int_blocks[ids].astype(jnp.float32)
        product = jnp.einsum("rik,rkj->rij", pieces, chosen).reshape(V, V).astype(jnp.bfloat16)
        left = amp_one.reshape(N_INTS, row_share, V).astype(jnp.float32)
        right = product.reshape(N_INTS, row_share, V).astype(jnp.float32)
        partials = jnp.einsum("qac,qad->qcd", left, right).astype(jnp.bfloat16)
        partials = lax.optimization_barrier(partials).astype(jnp.float32)
        return jnp.sum(partials, axis=0).astype(jnp.bfloat16)

    intermed = lax.map(pair_terms, (amp_half, block_ids))
    source = share_owner[:, 0].reshape(PAIRS, NSH) * PAIR_DEV + share_pair[:, 0].reshape(PAIRS, NSH)
    home = (jnp.arange(PAIRS, dtype=jnp.int32) // PAIR_DEV)[:, None] * PAIR_DEV + share_amp[:, 0].reshape(PAIRS, NSH)

    def cycle_one(packed):
        src, amp_index = packed
        return jnp.einsum("kac,kcb->ab", intermed[src].astype(jnp.float32), amp_half[amp_index].astype(jnp.float32))

    cycle_term = lax.map(cycle_one, (source, home))
    divisor = virt_energy[:, :, None] + virt_energy[:, None, :] - pair_energy[:, None, None]
    scaled = (resid_rest + cycle_term) / divisor
    return -0.5 * (scaled + jnp.transpose(scaled[transpose_pair], (0, 2, 1)))
```

```python
import functools

import jax
import jax.numpy as jnp
from jax import lax
from jax.experimental import pallas as pl
from jax.experimental.pallas import tpu as pltpu
from jax.sharding import PartitionSpec as P

F32, BF16 = jnp.float32, jnp.bfloat16
DIRECT = 16
NT = (((1,), (1,)), ((), ()))
TN = (((0,), (0,)), ((), ()))


def dot(a, b, dims=(((1,), (0,)), ((), ()))):
    return lax.dot_general(a, b, dims, preferred_element_type=F32)


def iota(shape, dim):
    return lax.broadcasted_iota(jnp.int32, shape, dim)


def partner(value, axis, offset):
    count = lax.axis_size(axis)
    return lax.ppermute(value, axis, [(source, source ^ offset) for source in range(count)])


def gathered(value, axis):
    count = lax.axis_size(axis)
    if count > DIRECT:
        return [lax.all_gather(value, axis, axis=0, tiled=False)]
    return [value] + [partner(value, axis, offset) for offset in range(1, count)]


def prepare(amps, resid, block, virt, pair, items, owners, wanted, share, rows_out, bt_out, far_out):
    pairs, height, domain = amps.shape
    quarter = lax.axis_index("ints")
    rows = pairs * height
    amp_half = amps[...].astype(BF16)
    rows_out[:, :, :domain] = amp_half
    n_items = items.shape[1]
    lanes = rows_out.shape[2] - domain
    spread = (iota((rows, n_items), 0) * n_items // rows == iota((rows, n_items), 1)).astype(BF16)
    named = jnp.broadcast_to(items[...].astype(F32), (lanes, n_items)).astype(BF16)
    rows_out[:, :, domain:] = dot(spread, named, NT).astype(BF16).reshape(pairs, height, lanes)

    chosen = (iota((height, domain), 1) == iota((height, domain), 0) + quarter * height).astype(BF16)
    bt_out[...] = dot(chosen, block[0], NT).astype(BF16)

    far_out[:rows, :] = amp_half.reshape(rows, domain)
    far_out[rows : 2 * rows, :] = resid[...].astype(BF16).reshape(rows, domain)
    n_req = owners.shape[1]
    source = owners[...] * pairs + wanted[...]
    hits = (source == iota((domain, n_req), 0)).astype(BF16)
    row, col = iota((8, n_req), 0), iota((8, n_req), 1)
    into = ((col // (n_req // pairs) == row // pairs) & (share[...] == row % pairs)).astype(BF16)
    counts = dot(into, hits, NT)
    row = iota((8, domain), 0)
    energy = jnp.zeros((8, domain), F32)
    for p in range(pairs):
        energy = jnp.where(row == p, virt[p : p + 1, :], energy)
        energy = jnp.where(row == pairs + p, pair[p], energy)
    high = energy.astype(BF16).astype(F32)
    middle = (energy - high).astype(BF16).astype(F32)
    low = energy - high - middle
    far_out[2 * rows :, :] = jnp.concatenate([counts, high, middle, low], axis=0).astype(BF16)


def intermediate(n_rows, *refs):
    pieces, blocks, out = refs[:n_rows], refs[n_rows:-1], refs[-1]
    pairs, height, _ = pieces[0].shape
    domain = blocks[0].shape[-1]
    group = lax.axis_index("pairs")
    x = [jnp.concatenate([piece[p, :, :domain] for piece in pieces], axis=0) for p in range(pairs)]
    x_all = jnp.concatenate(x, axis=0)
    ids = jnp.concatenate([piece[p, :, domain:] for p in range(pairs) for piece in pieces], axis=0)
    ids = ids.astype(F32).astype(jnp.int32)
    total, lanes = x_all.shape[0], 2 * height
    first = iota((total, lanes), 1) < height

    def chosen(two, low, high):
        return jnp.where(ids == jnp.where(first, low, high), dot(x_all, two, NT), 0.0)

    if len(blocks) > 1:
        product = sum(
            chosen(jnp.concatenate([blocks[k][...], blocks[k + 1][...]], axis=0), group ^ k, group ^ (k + 1))
            for k in range(0, len(blocks), 2)
        )
    else:

        def step(k, sofar):
            two = blocks[0][pl.ds(2 * k, 2)].reshape(lanes, domain)
            return sofar + chosen(two, 2 * k, 2 * k + 1)

        product = lax.fori_loop(0, blocks[0].shape[0] // 2, step, jnp.zeros((total, lanes), F32))
    product = product.astype(BF16)
    for p in range(pairs):
        both = dot(product[p * domain : (p + 1) * domain], x[p], TN)
        out[p * height : (p + 1) * height, :] = (both[:height] + both[height:]).astype(BF16)


def cycle(n_sends, rows_own, resid, near, far, swap, *refs):
    units, (own_out, *sends), (here, there) = refs[: -n_sends - 3], refs[-n_sends - 3 : -2], refs[-2:]
    pairs, height, domain = resid.shape
    rows = pairs * height
    group, quarter = lax.axis_index("pairs"), lax.axis_index("ints")
    n_pairs = lax.axis_size("pairs")
    terms = pairs * pairs
    lanes = -(-n_pairs * pairs // 128) * 128
    counts = jnp.concatenate([near[2 * rows : 2 * rows + 8, :lanes], far[2 * rows : 2 * rows + 8, :lanes]], axis=0)
    tall = 2 * terms * height
    which = iota((tall, 16), 0) // height
    which = jnp.where(which < terms, which, which - terms + 8)
    spread = dot((which == iota((tall, 16), 1)).astype(BF16), counts).astype(BF16)
    same = iota((tall, rows), 0) % height == iota((tall, rows), 1) % height

    def weights(source_group):
        place = iota((lanes, rows), 0) == source_group * pairs + iota((lanes, rows), 1) // height
        return jnp.where(same, dot(spread, place.astype(BF16)), 0.0).astype(BF16)

    if len(units) > 1:
        mixed = sum(dot(weights(group ^ k), unit[...]) for k, unit in enumerate(units))
    else:
        mixed = lax.fori_loop(
            0,
            units[0].shape[0],
            lambda k, sofar: sofar + dot(weights(k), units[0][k]),
            jnp.zeros((tall, domain), F32),
        )
    mixed = mixed.astype(BF16)

    start = pl.multiple_of(quarter * height, height)
    amps_near = rows_own[:, :, :domain].reshape(rows, domain)
    amps_far = far[:rows, :]

    def fill(target, side, amps, packed, terms_of):
        parts = packed[2 * rows + 8 : 2 * rows + 32, :].astype(F32)
        energy = parts[:8] + parts[8:16] + parts[16:24]
        tall_energy = energy.T
        for p in range(pairs):
            at = (side * pairs + p) * rows
            target[p] = dot(mixed[at : at + rows], amps, TN)
            target[p, pl.ds(start, height), :] += terms_of(p)
            divisor = tall_energy[:, p : p + 1] + energy[p : p + 1] - energy[pairs + p : pairs + p + 1]
            target[p] = target[p] / divisor

    fill(there, 1, amps_far, far, lambda p: far[rows + p * height : rows + (p + 1) * height, :].astype(F32))
    fill(here, 0, amps_near, near, lambda p: resid[p])
    base = (group ^ (n_pairs // 2)) * pairs
    for p in range(pairs):
        here[p] += there[swap[p] - base].T
    own_out[...] = here[:, pl.ds(start, height), :]
    for offset, send in enumerate(sends, 1):
        to = pl.multiple_of((quarter ^ offset) * height, height)
        send[...] = here[:, pl.ds(to, height), :].astype(BF16)


VM = pl.BlockSpec(memory_space=pltpu.VMEM)
SM = pl.BlockSpec(memory_space=pltpu.SMEM)


def call(kernel, outs, in_specs, name, scratch=()):
    return pl.pallas_call(
        kernel,
        out_shape=outs,
        in_specs=in_specs,
        out_specs=jax.tree.map(lambda _: VM, outs),
        scratch_shapes=scratch,
        name=name,
        compiler_params=pltpu.CompilerParams(vmem_limit_bytes=48 * 1024 * 1024),
    )


def body(
    amps,
    resid_rest,
    int_blocks,
    virt_energy,
    pair_energy,
    item_block,
    share_owner,
    share_pair,
    share_amp,
    transpose_pair,
):
    n_pairs, n_ints = lax.axis_size("pairs"), lax.axis_size("ints")
    pairs, height, domain = amps.shape
    rows = pairs * height
    shape = jax.ShapeDtypeStruct
    rows_own, bt, near = call(
        prepare,
        [
            shape((pairs, height, domain + 128), BF16),
            shape((height, domain), BF16),
            shape((2 * rows + 32, domain), BF16),
        ],
        [VM, VM, VM, VM, SM, VM, VM, VM, VM],
        "prepare",
    )(
        amps,
        resid_rest,
        int_blocks,
        virt_energy,
        pair_energy,
        item_block.reshape(1, -1),
        share_owner.reshape(1, -1),
        share_pair.reshape(1, -1),
        share_amp.reshape(1, -1),
    )
    blocks = gathered(bt, "pairs")
    pieces = [rows_own] + [partner(rows_own, "ints", k) for k in range(1, n_ints)]
    far = partner(near, "pairs", n_pairs // 2)
    inter = call(
        functools.partial(intermediate, n_ints),
        shape((rows, domain), BF16),
        [VM] * (n_ints + len(blocks)),
        "intermediate",
    )(*pieces, *blocks)
    units = gathered(inter, "pairs")
    own, *sends = call(
        functools.partial(cycle, n_ints - 1),
        [shape((pairs, height, domain), F32)] + [shape((pairs, height, domain), BF16)] * (n_ints - 1),
        [VM, VM, VM, VM, SM] + [VM] * len(units),
        "cycle",
        [pltpu.VMEM((pairs, domain, domain), F32)] * 2,
    )(rows_own, resid_rest, near, far, transpose_pair, *units)
    for offset, send in enumerate(sends, 1):
        own = own + partner(send, "ints", offset).astype(F32)
    return -0.5 * own


def solution(mesh):
    placed = (
        P("pairs", "ints", None),
        P("pairs", "ints", None),
        P("pairs", None, None),
        P("pairs", None),
        P("pairs"),
        P(("pairs", "ints"), None),
        P("pairs", None),
        P("pairs", None),
        P("pairs", None),
        P("pairs"),
    )
    return jax.shard_map(
        body, mesh=mesh, in_specs=placed, out_specs=P("pairs", "ints", None), check_vma=False
    )
```

```python
import functools

import jax
import jax.numpy as jnp
from jax import lax
from jax.experimental import pallas as pl
from jax.experimental.pallas import tpu as pltpu
from jax.sharding import PartitionSpec as P

F32, BF16 = jnp.float32, jnp.bfloat16
DIRECT = 16
CORE = 1
NT = (((1,), (1,)), ((), ()))
TN = (((0,), (0,)), ((), ()))
TILE = 16


def dot(a, b, dims=(((1,), (0,)), ((), ()))):
    return lax.dot_general(a, b, dims, preferred_element_type=F32)


def iota(shape, dim):
    return lax.broadcasted_iota(jnp.int32, shape, dim)


def exchange(value, pair_offset, int_offset):
    n_pairs, n_ints = lax.axis_size("pairs"), lax.axis_size("ints")
    route = [
        (p * n_ints + q, (p ^ pair_offset) * n_ints + (q ^ int_offset)) for p in range(n_pairs) for q in range(n_ints)
    ]
    return lax.ppermute(value, ("pairs", "ints"), route)


def family_exchange(value, offset):
    n_pairs, n_ints = lax.axis_size("pairs"), lax.axis_size("ints")
    half = n_pairs // 2
    route = [
        (p * n_ints + q, (p ^ offset ^ (q % 2 * half)) * n_ints + q) for p in range(n_pairs) for q in range(n_ints)
    ]
    return lax.ppermute(value, ("pairs", "ints"), route)


def place():
    group, member, n_pairs = lax.axis_index("pairs"), lax.axis_index("ints"), lax.axis_size("pairs")
    core = member % 2
    return group, member, core, group ^ (core * (n_pairs // 2)), n_pairs // 2


def prepare(
    amps, block, resid, virt, pair, items, owners, wanted, share, lean_out, full_out, half_out, resid_out, *scratch
):
    hbm = (amps, block, resid, virt, pair, items, owners, wanted, share)
    held, sems = scratch[:-1], scratch[-1]
    copies = [pltpu.make_async_copy(src, dst, sems.at[i]) for i, (src, dst) in enumerate(zip(hbm, held))]
    for copy in copies:
        copy.start()
    amps, block, resid, virt, pair, items, owners, wanted, share = held
    pairs, height, domain = amps.shape
    rows = pairs * height
    member = lax.axis_index("ints")
    half_rows = half_out.shape[0]
    half_start = member // 2 * half_rows
    chosen = (iota((half_rows, domain), 1) == iota((half_rows, domain), 0) + half_start).astype(BF16)
    mine = (iota((height, domain), 1) == iota((height, domain), 0) + member * height).astype(BF16)

    for copy in copies[3:]:
        copy.wait()
    n_items, n_req = items.shape[1], owners.shape[1]
    named = jnp.concatenate(
        [jnp.broadcast_to(items[...].astype(F32), (TILE, n_items)), jnp.zeros((TILE, domain - n_items), F32)], axis=1
    ).astype(BF16)
    source = owners[...] * pairs + wanted[...]
    hits = (source == iota((domain, n_req), 0)).astype(BF16)
    row, col = iota((8, n_req), 0), iota((8, n_req), 1)
    into = ((col // (n_req // pairs) == row // pairs) & (share[...] == row % pairs)).astype(BF16)
    counts = dot(into, hits, NT)
    row = iota((8, domain), 0)
    energy = jnp.zeros((8, domain), F32)
    for p in range(pairs):
        energy = jnp.where(row == p, virt[p : p + 1, :], energy)
        energy = jnp.where(row == pairs + p, pair[p], energy)
    high = energy.astype(BF16).astype(F32)
    middle = (energy - high).astype(BF16).astype(F32)
    low = energy - high - middle
    full_out[rows + TILE + height :, :] = jnp.concatenate([counts, high, middle, low], axis=0).astype(BF16)
    lean_out[rows:, :] = named
    full_out[rows : rows + TILE, :] = named
    copies[0].wait()
    amp_half = amps[...].astype(BF16).reshape(rows, domain)
    lean_out[:rows, :] = amp_half
    full_out[:rows, :] = amp_half
    copies[1].wait()
    half_out[...] = dot(chosen, block[0], NT).astype(BF16)
    full_out[rows + TILE : rows + TILE + height, :] = dot(mine, block[0], NT).astype(BF16)
    copies[2].wait()
    resid_out[...] = resid[...].astype(BF16).reshape(rows, domain)


def ordered(core, own, other):
    return jnp.where(core == 0, own, other), jnp.where(core == 0, other, own)


def intermediate(n_shared, items, pairs, own, own_c, far, far_c, half_own, *refs):
    y_refs, rest, out = refs[: 4 * n_shared], refs[4 * n_shared : -1], refs[-1]
    half_rows, domain = half_own.shape
    height = half_rows // 2
    rows = pairs * height
    group, _, core, family, half = place()

    near = [own, own_c] + list(y_refs[: 2 * n_shared])
    away = [far, far_c] + list(y_refs[2 * n_shared :])
    lean = rows + TILE
    pieces = [jnp.where(core == 0, a[:lean, :], b[:lean, :]) for a, b in zip(near, away)]
    x = [jnp.concatenate([piece[p * height : (p + 1) * height] for piece in pieces], axis=0) for p in range(pairs)]
    x_all = jnp.concatenate(x, axis=0)
    spread = (iota((rows, domain), 0) * items // rows == iota((rows, domain), 1)).astype(BF16)
    named = [dot(spread, jnp.broadcast_to(piece[rows : rows + 1], (half_rows, domain)), NT) for piece in pieces]
    ids = jnp.concatenate(
        [name[p * height : (p + 1) * height] for p in range(pairs) for name in named], axis=0
    ).astype(jnp.int32)

    def chosen(block, index):
        return jnp.where(ids == index, dot(x_all, block, NT), 0.0)

    if len(rest) > 1:
        count = len(rest) // 2
        near_quarter = far[lean : lean + height, :]
        away_quarter = far_c[lean : lean + height, :]
        product = chosen(half_own[...], group)
        product += chosen(jnp.concatenate(ordered(core, near_quarter, away_quarter), axis=0), group ^ half)
        for j in range(count):
            product += chosen(rest[j][...], family ^ (j + 1))
            product += chosen(rest[count + j][...], family ^ half ^ (j + 1))
    else:
        product = lax.fori_loop(
            0,
            rest[0].shape[0],
            lambda k, sofar: sofar + chosen(rest[0][k], k),
            jnp.zeros((pairs * domain, half_rows), F32),
        )
    product = product.astype(BF16)
    for p in range(pairs):
        both = dot(product[p * domain : (p + 1) * domain], x[p], TN)
        out[p * half_rows : (p + 1) * half_rows, :] = both.astype(BF16)


def spread_counts(own, far, swaps, half_rows, lanes):
    start, pairs = own.shape[0] - 32, len(swaps)
    counts = jnp.concatenate([own[start : start + 8, :lanes], far[start : start + 8, :lanes]], axis=0)
    tall = 2 * pairs * pairs * half_rows
    term = iota((tall, 16), 0) // half_rows
    which = term
    for p, swap in enumerate(swaps):
        which = jnp.where(term // pairs == pairs + p, 8 + swap * pairs + term % pairs, which)
    return dot((which == iota((tall, 16), 1)).astype(BF16), counts).astype(BF16)


def weights(spread, source_group, pairs, half_rows):
    tall, lanes = spread.shape
    wide = pairs * half_rows
    same = iota((tall, wide), 0) % half_rows == iota((tall, wide), 1) % half_rows
    place_of = iota((lanes, wide), 0) == source_group * pairs + iota((lanes, wide), 1) // half_rows
    return jnp.where(same, dot(spread, place_of.astype(BF16)), 0.0).astype(BF16)


def lanes_of(pairs):
    return -(-lax.axis_size("pairs") * pairs // 128) * 128


def factors(n_units, resid, own, far, swap, weights_out, inverse_out, base_out, swap_out, *scratch):
    held, sems = scratch[:-1], scratch[-1]
    copies = [pltpu.make_async_copy(src, dst, sems.at[i]) for i, (src, dst) in enumerate(zip((resid, swap), held))]
    for copy in copies:
        copy.start()
    resid, swap = held
    pairs, height, domain = resid.shape
    half_rows = 2 * height
    wide = pairs * half_rows
    group, member, _, family, half = place()
    for copy in copies:
        copy.wait()
    swaps = [swap[p] - (group ^ half) * pairs for p in range(pairs)]
    spread = spread_counts(own, far, swaps, half_rows, lanes_of(pairs))
    for k in range(n_units):
        weights_out[:, k * wide : (k + 1) * wide] = weights(spread, family ^ k, pairs, half_rows)
    start = own.shape[0] - 24

    def energy_of(packed):
        parts = packed[start : start + 24, :].astype(F32)
        energy = parts[:8] + parts[8:16] + parts[16:24]
        return energy, energy.T

    def inverse(energy, tall_energy, p):
        divisor = tall_energy[:, p : p + 1] + energy[p : p + 1] - energy[pairs + p : pairs + p + 1]
        return 1.0 / divisor

    near, away = energy_of(own), energy_of(far)
    away = [inverse(*away, p) for p in range(pairs)]
    for p in range(pairs):
        inverse_out[p] = inverse(*near, p)
        inverse_out[pairs + p] = functools.reduce(
            lambda kept, k: jnp.where(swaps[p] == k, away[k], kept), range(1, pairs), away[0]
        )
        swap_out[p] = jnp.full(swap_out.shape[1:], swaps[p], jnp.int32)
    rows = pl.ds(pl.multiple_of(member * height, height), height)
    base_out[...] = resid[...] * inverse_out[:pairs, rows, :]


def cycle(n_sends, pairs, own, own_c, far, far_c, resid_far, mix, inverse, base, swap, *refs):
    units, (own_out, *sends), (here, there) = refs[: -n_sends - 3], refs[-n_sends - 3 : -2], refs[-2:]
    height, domain = resid_far.shape[0] // pairs, resid_far.shape[1]
    rows = pairs * height
    half_rows = 2 * height
    group, member, core, family, half = place()
    if len(units) > 1:
        mixed = dot(mix[...], jnp.concatenate([unit[...] for unit in units], axis=0))
    else:
        swaps = [swap[p, :1, :1] for p in range(pairs)]
        spread = spread_counts(own, far, swaps, half_rows, lanes_of(pairs))
        first = group - group % half
        mixed = lax.fori_loop(
            0,
            units[0].shape[0],
            lambda k, sofar: sofar
            + dot(weights(spread, (first + k) ^ (core * half), pairs, half_rows), units[0][k]),
            jnp.zeros((spread.shape[0], domain), F32),
        )
    mixed = mixed.astype(BF16)
    start = pl.ds(pl.multiple_of(member * height, height), height)

    def amps_of(mine, other):
        low, high = ordered(core, mine[:rows, :], other[:rows, :])
        return jnp.concatenate(
            [part[p * height : (p + 1) * height] for p in range(pairs) for part in (low, high)], axis=0
        )

    wide = pairs * half_rows
    near, away = amps_of(own, own_c), amps_of(far, far_c)
    for p in range(pairs):
        at = (pairs + p) * wide
        there[...] = dot(mixed[at : at + wide], away, TN)
        parts = [resid_far[k * height : (k + 1) * height, :].astype(F32) for k in range(pairs)]
        named = swap[p, :1, :1]
        there[start, :] += functools.reduce(
            lambda kept, k: jnp.where(named == k, parts[k], kept), range(1, pairs), parts[0]
        )
        mirror = (there[...] * inverse[pairs + p]).T
        at = p * wide
        here[p] = dot(mixed[at : at + wide], near, TN) * inverse[p] + mirror
    own_out[...] = here[:, start, :] + base[...]
    for offset, send in enumerate(sends, 1):
        to = pl.multiple_of((member ^ offset) * height, height)
        send[...] = here[:, pl.ds(to, height), :].astype(BF16)


VM = pl.BlockSpec(memory_space=pltpu.VMEM)
HB = pl.BlockSpec(memory_space=pltpu.HBM)


def stay(value):
    return pltpu.with_memory_space_constraint(value, pltpu.HBM)


def call(kernel, outs, in_specs, name, scratch=()):
    return pl.pallas_call(
        kernel,
        out_shape=outs,
        in_specs=in_specs,
        out_specs=jax.tree.map(lambda _: VM, outs),
        scratch_shapes=scratch,
        name=name,
        compiler_params=pltpu.CompilerParams(vmem_limit_bytes=48 * 1024 * 1024),
    )


def body(
    amps,
    resid_rest,
    int_blocks,
    virt_energy,
    pair_energy,
    item_block,
    share_owner,
    share_pair,
    share_amp,
    transpose_pair,
):
    n_pairs, n_ints = lax.axis_size("pairs"), lax.axis_size("ints")
    pairs, height, domain = amps.shape
    rows, half_rows, half = pairs * height, 2 * height, n_pairs // 2
    shape = jax.ShapeDtypeStruct
    operands = (
        amps,
        int_blocks,
        resid_rest,
        virt_energy,
        pair_energy,
        item_block.reshape(1, -1),
        share_owner.reshape(1, -1),
        share_pair.reshape(1, -1),
        share_amp.reshape(1, -1),
    )
    lean, own, half_own, resid_half = call(
        prepare,
        [
            shape((rows + TILE, domain), BF16),
            shape((rows + TILE + height + 32, domain), BF16),
            shape((half_rows, domain), BF16),
            shape((rows, domain), BF16),
        ],
        [HB] * len(operands),
        "prepare",
        [(pltpu.SMEM if o is pair_energy else pltpu.VMEM)(o.shape, o.dtype) for o in operands]
        + [pltpu.SemaphoreType.DMA((len(operands),))],
    )(*map(stay, operands))
    far = exchange(own, half, 0)
    y_own = [exchange(lean, 0, k) for k in range(2, n_ints, 2)]
    y_far = [exchange(lean, half, k) for k in range(2, n_ints, 2)]
    across = lambda value: exchange(value, 0, CORE)
    own_c, far_c = across(lean), across(far)
    if n_pairs <= DIRECT:
        blocks = [family_exchange(half_own, j) for j in range(1, half)]
        blocks += [across(block) for block in blocks]
    else:
        blocks = [lax.all_gather(half_own, "pairs", axis=0, tiled=False)]
    near_rows = [v for y in y_own for v in (y, across(y))]
    away_rows = [v for y in y_far for v in (y, across(y))]
    inter = call(
        functools.partial(intermediate, len(y_own), item_block.shape[0], pairs),
        shape((pairs * half_rows, domain), BF16),
        [VM] * (5 + len(near_rows) + len(away_rows) + len(blocks)),
        "intermediate",
    )(own, own_c, far, far_c, half_own, *near_rows, *away_rows, *blocks)
    if n_pairs <= DIRECT:
        units = [inter] + [exchange(inter, j, 0) for j in range(1, half)]
    else:
        every = lax.all_gather(inter, "pairs", axis=0, tiled=False)
        first = lax.axis_index("pairs") // half * half
        units = [lax.dynamic_slice_in_dim(every, first, half, 0)]
    resid_far = exchange(resid_half, half, 0)
    n_units = len(units)
    mix, inverse, base, swap = call(
        functools.partial(factors, n_units if n_units > 1 else 0),
        [
            shape((2 * pairs * pairs * half_rows, n_units * pairs * half_rows), BF16),
            shape((2 * pairs, domain, domain), F32),
            shape((pairs, height, domain), F32),
            shape((pairs, 8, 128), jnp.int32),
        ],
        [HB, VM, VM, HB],
        "factors",
        [
            pltpu.VMEM(resid_rest.shape, F32),
            pltpu.SMEM(transpose_pair.shape, jnp.int32),
            pltpu.SemaphoreType.DMA((2,)),
        ],
    )(stay(resid_rest), own, far, stay(transpose_pair))
    mine, *sends = call(
        functools.partial(cycle, n_ints - 1, pairs),
        [shape((pairs, height, domain), F32)] + [shape((pairs, height, domain), BF16)] * (n_ints - 1),
        [VM] * (9 + n_units),
        "cycle",
        [pltpu.VMEM((pairs, domain, domain), F32), pltpu.VMEM((domain, domain), F32)],
    )(own, own_c, far, far_c, resid_far, mix, inverse, base, swap, *units)
    for offset, send in enumerate(sends, 1):
        mine = mine + exchange(send, 0, offset).astype(F32)
    return -0.5 * mine


def solution(mesh):
    placed = (
        P("pairs", "ints", None),
        P("pairs", "ints", None),
        P("pairs", None, None),
        P("pairs", None),
        P("pairs"),
        P(("pairs", "ints"), None),
        P("pairs", None),
        P("pairs", None),
        P("pairs", None),
        P("pairs"),
    )
    return jax.shard_map(
        body, mesh=mesh, in_specs=placed, out_specs=P("pairs", "ints", None), check_vma=False
    )
```

```python
import functools

import jax
import jax.numpy as jnp
from jax import lax
from jax.experimental import pallas as pl
from jax.experimental.pallas import tpu as pltpu
from jax.sharding import PartitionSpec as P

F32, BF16 = jnp.float32, jnp.bfloat16
DIRECT = 16
CORE = 1
NT = (((1,), (1,)), ((), ()))
TN = (((0,), (0,)), ((), ()))
TILE = 16


def dot(a, b, dims=(((1,), (0,)), ((), ()))):
    return lax.dot_general(a, b, dims, preferred_element_type=F32)


def iota(shape, dim):
    return lax.broadcasted_iota(jnp.int32, shape, dim)


def exchange(value, pair_offset, int_offset):
    n_pairs, n_ints = lax.axis_size("pairs"), lax.axis_size("ints")
    route = [
        (p * n_ints + q, (p ^ pair_offset) * n_ints + (q ^ int_offset)) for p in range(n_pairs) for q in range(n_ints)
    ]
    return lax.ppermute(value, ("pairs", "ints"), route)


def family_exchange(value, offset):
    n_pairs, n_ints = lax.axis_size("pairs"), lax.axis_size("ints")
    half = n_pairs // 2
    route = [
        (p * n_ints + q, (p ^ offset ^ (q % 2 * half)) * n_ints + q) for p in range(n_pairs) for q in range(n_ints)
    ]
    return lax.ppermute(value, ("pairs", "ints"), route)


def place():
    group, member, n_pairs = lax.axis_index("pairs"), lax.axis_index("ints"), lax.axis_size("pairs")
    core = member % 2
    return group, member, core, group ^ (core * (n_pairs // 2)), n_pairs // 2


def prepare(
    amps, block, resid, virt, pair, items, owners, wanted, share, lean_out, half_out, tail_out, resid_out, *scratch
):
    hbm = (amps, block, resid, virt, pair, items, owners, wanted, share)
    held, sems = scratch[:-1], scratch[-1]
    copies = [pltpu.make_async_copy(src, dst, sems.at[i]) for i, (src, dst) in enumerate(zip(hbm, held))]
    for copy in copies:
        copy.start()
    amps, block, resid, virt, pair, items, owners, wanted, share = held
    pairs, height, domain = amps.shape
    rows = pairs * height
    member = lax.axis_index("ints")
    half_rows = half_out.shape[0]
    half_start = member // 2 * half_rows
    chosen = (iota((half_rows, domain), 1) == iota((half_rows, domain), 0) + half_start).astype(BF16)
    mine = (iota((height, domain), 1) == iota((height, domain), 0) + member * height).astype(BF16)

    for copy in copies[3:]:
        copy.wait()
    n_items, n_req = items.shape[1], owners.shape[1]
    named = jnp.concatenate(
        [jnp.broadcast_to(items[...].astype(F32), (TILE, n_items)), jnp.zeros((TILE, domain - n_items), F32)], axis=1
    ).astype(BF16)
    source = owners[...] * pairs + wanted[...]
    hits = (source == iota((domain, n_req), 0)).astype(BF16)
    row, col = iota((TILE, n_req), 0), iota((TILE, n_req), 1)
    into = ((col // (n_req // pairs) == row // pairs) & (share[...] == row % pairs)).astype(BF16)
    extras = dot(into, hits, NT)
    terms, lines = pairs * pairs, 2 * pairs
    row = iota((TILE, domain), 0)
    line = (row - terms) % lines
    energy = jnp.zeros((TILE, domain), F32)
    for p in range(pairs):
        energy = jnp.where(line == p, virt[p : p + 1, :], energy)
        energy = jnp.where(line == pairs + p, pair[p], energy)
    high = energy.astype(BF16).astype(F32)
    middle = (energy - high).astype(BF16).astype(F32)
    low = energy - high - middle
    for k, part in enumerate((high, middle, low)):
        extras = jnp.where((row - terms) // lines == k, jnp.where(row >= terms, part, extras), extras)
    tail_out[:TILE, :] = extras.astype(BF16)
    lean_out[rows:, :] = named
    copies[0].wait()
    amp_half = amps[...].astype(BF16).reshape(rows, domain)
    lean_out[:rows, :] = amp_half
    copies[1].wait()
    half_out[...] = dot(chosen, block[0], NT).astype(BF16)
    tail_out[TILE:, :] = dot(mine, block[0], NT).astype(BF16)
    copies[2].wait()
    resid_out[...] = resid[...].astype(BF16).reshape(rows, domain)


def ordered(core, own, other):
    return jnp.where(core == 0, own, other), jnp.where(core == 0, other, own)


def intermediate(n_shared, items, pairs, own, own_c, far, far_c, far_tail, far_tail_c, half_own, *refs):
    y_refs, rest, out = refs[: 4 * n_shared], refs[4 * n_shared : -1], refs[-1]
    half_rows, domain = half_own.shape
    height = half_rows // 2
    rows = pairs * height
    group, _, core, family, half = place()

    near = [own, own_c] + list(y_refs[: 2 * n_shared])
    away = [far, far_c] + list(y_refs[2 * n_shared :])
    lean = rows + TILE
    pieces = [jnp.where(core == 0, a[:lean, :], b[:lean, :]) for a, b in zip(near, away)]
    x = [jnp.concatenate([piece[p * height : (p + 1) * height] for piece in pieces], axis=0) for p in range(pairs)]
    x_all = jnp.concatenate(x, axis=0)
    spread = (iota((rows, domain), 0) * items // rows == iota((rows, domain), 1)).astype(BF16)
    named = [dot(spread, jnp.broadcast_to(piece[rows : rows + 1], (half_rows, domain)), NT) for piece in pieces]
    ids = jnp.concatenate(
        [name[p * height : (p + 1) * height] for p in range(pairs) for name in named], axis=0
    ).astype(jnp.int32)

    def chosen(block, index):
        return jnp.where(ids == index, dot(x_all, block, NT), 0.0)

    if len(rest) > 1:
        count = len(rest) // 2
        product = chosen(half_own[...], group)
        product += chosen(jnp.concatenate(ordered(core, far_tail[TILE:, :], far_tail_c[TILE:, :]), axis=0), group ^ half)
        for j in range(count):
            product += chosen(rest[j][...], family ^ (j + 1))
            product += chosen(rest[count + j][...], family ^ half ^ (j + 1))
    else:
        product = lax.fori_loop(
            0,
            rest[0].shape[0],
            lambda k, sofar: sofar + chosen(rest[0][k], k),
            jnp.zeros((pairs * domain, half_rows), F32),
        )
    product = product.astype(BF16)
    for p in range(pairs):
        both = dot(product[p * domain : (p + 1) * domain], x[p], TN)
        out[p * half_rows : (p + 1) * half_rows, :] = both.astype(BF16)


def spread_counts(own, far, swaps, half_rows, lanes):
    pairs = len(swaps)
    counts = jnp.concatenate([own[:TILE, :lanes], far[:TILE, :lanes]], axis=0)
    tall = 2 * pairs * pairs * half_rows
    term = iota((tall, 2 * TILE), 0) // half_rows
    which = term
    for p, swap in enumerate(swaps):
        which = jnp.where(term // pairs == pairs + p, TILE + swap * pairs + term % pairs, which)
    return dot((which == iota((tall, 2 * TILE), 1)).astype(BF16), counts).astype(BF16)


def weights(spread, source_group, pairs, half_rows):
    tall, lanes = spread.shape
    wide = pairs * half_rows
    same = iota((tall, wide), 0) % half_rows == iota((tall, wide), 1) % half_rows
    place_of = iota((lanes, wide), 0) == source_group * pairs + iota((lanes, wide), 1) // half_rows
    return jnp.where(same, dot(spread, place_of.astype(BF16)), 0.0).astype(BF16)


def lanes_of(pairs):
    return -(-lax.axis_size("pairs") * pairs // 128) * 128


def energies(packed, pairs):
    parts, lines, start = packed[:TILE, :].astype(F32), 2 * pairs, pairs * pairs
    energy = parts[start : start + lines]
    for k in (1, 2):
        energy += parts[start + k * lines : start + (k + 1) * lines]
    energy = jnp.concatenate([energy, jnp.zeros((8 - lines, energy.shape[1]), F32)], axis=0)
    return energy, energy.T


def inverse_of(energy, tall_energy, p, pairs):
    return 1.0 / (tall_energy[:, p : p + 1] + energy[p : p + 1] - energy[pairs + p : pairs + p + 1])


def near_factors(resid, own, inverse_out, base_out, held, sem):
    copy = pltpu.make_async_copy(resid, held, sem)
    copy.start()
    pairs, height, _ = resid.shape
    near = energies(own, pairs)
    for p in range(pairs):
        inverse_out[p] = inverse_of(*near, p, pairs)
    start = pl.multiple_of(lax.axis_index("ints") * height, height)
    copy.wait()
    base_out[...] = held[...] * inverse_out[:, pl.ds(start, height), :]


def factors(n_units, pairs, own, far, swap, weights_out, inverse_out, swap_out, held, sem):
    copy = pltpu.make_async_copy(swap, held, sem)
    copy.start()
    half_rows = weights_out.shape[0] // (2 * pairs * pairs)
    wide = pairs * half_rows
    group, _, _, family, half = place()
    away = energies(far, pairs)
    away = [inverse_of(*away, p, pairs) for p in range(pairs)]
    copy.wait()
    swaps = [held[p] - (group ^ half) * pairs for p in range(pairs)]
    spread = spread_counts(own, far, swaps, half_rows, lanes_of(pairs))
    for k in range(n_units):
        weights_out[:, k * wide : (k + 1) * wide] = weights(spread, family ^ k, pairs, half_rows)
    for p in range(pairs):
        inverse_out[p] = functools.reduce(
            lambda kept, k: jnp.where(swaps[p] == k, away[k], kept), range(1, pairs), away[0]
        )
        swap_out[p] = jnp.full(swap_out.shape[1:], swaps[p], jnp.int32)


def cycle(n_sends, pairs, own, own_c, far, far_c, tail, far_tail, resid_far, mix, inverse, inverse_far, base, swap, *refs):
    units, (own_out, *sends), (here, there) = refs[: -n_sends - 3], refs[-n_sends - 3 : -2], refs[-2:]
    height, domain = base.shape[1:]
    rows = pairs * height
    half_rows = 2 * height
    group, member, core, family, half = place()
    if len(units) > 1:
        mixed = dot(mix[...], jnp.concatenate([unit[...] for unit in units], axis=0))
    else:
        swaps = [swap[p, :1, :1] for p in range(pairs)]
        spread = spread_counts(tail, far_tail, swaps, half_rows, lanes_of(pairs))
        first = group - group % half
        mixed = lax.fori_loop(
            0,
            units[0].shape[0],
            lambda k, sofar: sofar
            + dot(weights(spread, (first + k) ^ (core * half), pairs, half_rows), units[0][k]),
            jnp.zeros((spread.shape[0], domain), F32),
        )
    mixed = mixed.astype(BF16)
    start = pl.ds(pl.multiple_of(member * height, height), height)

    def amps_of(mine, other):
        low, high = ordered(core, mine[:rows, :], other[:rows, :])
        return jnp.concatenate(
            [part[p * height : (p + 1) * height] for p in range(pairs) for part in (low, high)], axis=0
        )

    wide = pairs * half_rows
    near, away = amps_of(own, own_c), amps_of(far, far_c)
    for p in range(pairs):
        at = (pairs + p) * wide
        there[...] = dot(mixed[at : at + wide], away, TN)
        parts = [resid_far[k * height : (k + 1) * height, :].astype(F32) for k in range(pairs)]
        named = swap[p, :1, :1]
        there[start, :] += functools.reduce(
            lambda kept, k: jnp.where(named == k, parts[k], kept), range(1, pairs), parts[0]
        )
        mirror = (there[...] * inverse_far[p]).T
        at = p * wide
        here[p] = dot(mixed[at : at + wide], near, TN) * inverse[p] + mirror
    own_out[...] = here[:, start, :] + base[...]
    for offset, send in enumerate(sends, 1):
        to = pl.multiple_of((member ^ offset) * height, height)
        send[...] = here[:, pl.ds(to, height), :].astype(BF16)


VM = pl.BlockSpec(memory_space=pltpu.VMEM)
HB = pl.BlockSpec(memory_space=pltpu.HBM)


def after(value, *others):
    return lax.optimization_barrier((value, *others))[0] if others else value


def stay(value):
    return pltpu.with_memory_space_constraint(value, pltpu.HBM)


def call(kernel, outs, in_specs, name, scratch=(), flops=0):
    return pl.pallas_call(
        kernel,
        out_shape=outs,
        in_specs=in_specs,
        out_specs=jax.tree.map(lambda _: VM, outs),
        scratch_shapes=scratch,
        name=name,
        cost_estimate=pl.CostEstimate(flops=flops, bytes_accessed=0, transcendentals=0) if flops else None,
        compiler_params=pltpu.CompilerParams(vmem_limit_bytes=48 * 1024 * 1024),
    )


def body(
    amps,
    resid_rest,
    int_blocks,
    virt_energy,
    pair_energy,
    item_block,
    share_owner,
    share_pair,
    share_amp,
    transpose_pair,
):
    n_pairs, n_ints = lax.axis_size("pairs"), lax.axis_size("ints")
    pairs, height, domain = amps.shape
    rows, half_rows, half = pairs * height, 2 * height, n_pairs // 2
    shape = jax.ShapeDtypeStruct
    operands = (
        amps,
        int_blocks,
        resid_rest,
        virt_energy,
        pair_energy,
        item_block.reshape(1, -1),
        share_owner.reshape(1, -1),
        share_pair.reshape(1, -1),
        share_amp.reshape(1, -1),
    )
    lean, half_own, tail, resid_half = call(
        prepare,
        [
            shape((rows + TILE, domain), BF16),
            shape((half_rows, domain), BF16),
            shape((TILE + height, domain), BF16),
            shape((rows, domain), BF16),
        ],
        [HB] * len(operands),
        "prepare",
        [(pltpu.SMEM if o is pair_energy else pltpu.VMEM)(o.shape, o.dtype) for o in operands]
        + [pltpu.SemaphoreType.DMA((len(operands),))],
    )(*map(stay, operands))
    inverse, base = call(
        near_factors,
        [shape((pairs, domain, domain), F32), shape((pairs, height, domain), F32)],
        [HB, VM],
        "near_factors",
        [pltpu.VMEM(resid_rest.shape, F32), pltpu.SemaphoreType.DMA],
        10**9,
    )(stay(resid_rest), tail)

    def across(value, *others):
        return exchange(after(value, *others), 0, CORE)

    far, far_tail = exchange(lean, half, 0), exchange(tail, half, 0)
    y_own = [exchange(lean, 0, k) for k in range(2, n_ints, 2)]
    blocks = [family_exchange(half_own, j) for j in range(1, half)] if n_pairs <= DIRECT else []
    y_far = [exchange(after(far, *y_own), 0, k) for k in range(2, n_ints, 2)]
    lead = blocks[:1]
    own_c, far_c = across(lean, *lead), across(far)
    far_tail_c = across(far_tail)
    if n_pairs <= DIRECT:
        blocks += [across(block) for block in blocks]
    else:
        blocks = [lax.all_gather(half_own, "pairs", axis=0, tiled=False)]
    near_rows = [v for y in y_own for v in (y, across(y, *lead))]
    away_rows = [v for y in y_far for v in (y, across(y))]
    inter = call(
        functools.partial(intermediate, len(y_own), item_block.shape[0], pairs),
        shape((pairs * half_rows, domain), BF16),
        [VM] * (7 + len(near_rows) + len(away_rows) + len(blocks)),
        "intermediate",
    )(lean, own_c, far, far_c, far_tail, far_tail_c, half_own, *near_rows, *away_rows, *blocks)
    if n_pairs <= DIRECT:
        units = [inter] + [exchange(inter, j, 0) for j in range(1, half)]
    else:
        every = lax.all_gather(inter, "pairs", axis=0, tiled=False)
        first = lax.axis_index("pairs") // half * half
        units = [lax.dynamic_slice_in_dim(every, first, half, 0)]
    resid_far = exchange(resid_half, half, 0)
    n_units = len(units)
    mix, inverse_far, swap = call(
        functools.partial(factors, n_units if n_units > 1 else 0, pairs),
        [
            shape((2 * pairs * pairs * half_rows, n_units * pairs * half_rows), BF16),
            shape((pairs, domain, domain), F32),
            shape((pairs, 8, 128), jnp.int32),
        ],
        [VM, VM, HB],
        "factors",
        [pltpu.SMEM(transpose_pair.shape, jnp.int32), pltpu.SemaphoreType.DMA],
    )(tail, far_tail, stay(transpose_pair))
    mine, *sends = call(
        functools.partial(cycle, n_ints - 1, pairs),
        [shape((pairs, height, domain), F32)] + [shape((pairs, height, domain), BF16)] * (n_ints - 1),
        [VM] * (12 + n_units),
        "cycle",
        [pltpu.VMEM((pairs, domain, domain), F32), pltpu.VMEM((domain, domain), F32)],
    )(lean, own_c, far, far_c, tail, far_tail, resid_far, mix, inverse, inverse_far, base, swap, *units)
    for offset, send in enumerate(sends, 1):
        mine = mine + exchange(send, 0, offset).astype(F32)
    return -0.5 * mine


def solution(mesh):
    placed = (
        P("pairs", "ints", None),
        P("pairs", "ints", None),
        P("pairs", None, None),
        P("pairs", None),
        P("pairs"),
        P(("pairs", "ints"), None),
        P("pairs", None),
        P("pairs", None),
        P("pairs", None),
        P("pairs"),
    )
    return jax.shard_map(
        body, mesh=mesh, in_specs=placed, out_specs=P("pairs", "ints", None), check_vma=False
    )
```

```python
import functools

import jax
import jax.numpy as jnp
from jax import lax
from jax.experimental import pallas as pl
from jax.experimental.pallas import tpu as pltpu
from jax.sharding import PartitionSpec as P

F32, BF16 = jnp.float32, jnp.bfloat16
DIRECT = 16
CORE = 1
NT = (((1,), (1,)), ((), ()))
TN = (((0,), (0,)), ((), ()))
TILE = 16


def dot(a, b, dims=(((1,), (0,)), ((), ()))):
    return lax.dot_general(a, b, dims, preferred_element_type=F32)


def iota(shape, dim):
    return lax.broadcasted_iota(jnp.int32, shape, dim)


def exchange(value, pair_offset, int_offset):
    n_pairs, n_ints = lax.axis_size("pairs"), lax.axis_size("ints")
    route = [
        (p * n_ints + q, (p ^ pair_offset) * n_ints + (q ^ int_offset)) for p in range(n_pairs) for q in range(n_ints)
    ]
    return lax.ppermute(value, ("pairs", "ints"), route)


def family_exchange(value, offset):
    n_pairs, n_ints = lax.axis_size("pairs"), lax.axis_size("ints")
    half = n_pairs // 2
    route = [
        (p * n_ints + q, (p ^ offset ^ (q % 2 * half)) * n_ints + q) for p in range(n_pairs) for q in range(n_ints)
    ]
    return lax.ppermute(value, ("pairs", "ints"), route)


def place():
    group, member, n_pairs = lax.axis_index("pairs"), lax.axis_index("ints"), lax.axis_size("pairs")
    core = member % 2
    return group, member, core, group ^ (core * (n_pairs // 2)), n_pairs // 2


def prepare(
    amps, block, resid, virt, pair, items, owners, wanted, share, lean_out, half_out, tail_out, resid_out, *scratch
):
    hbm = (amps, block, resid, virt, pair, items, owners, wanted, share)
    held, sems = scratch[:-1], scratch[-1]
    copies = [pltpu.make_async_copy(src, dst, sems.at[i]) for i, (src, dst) in enumerate(zip(hbm, held))]
    for copy in copies:
        copy.start()
    amps, block, resid, virt, pair, items, owners, wanted, share = held
    pairs, height, domain = amps.shape
    rows = pairs * height
    member = lax.axis_index("ints")
    half_rows = half_out.shape[0]
    half_start = member // 2 * half_rows
    chosen = (iota((half_rows, domain), 1) == iota((half_rows, domain), 0) + half_start).astype(BF16)
    mine = (iota((height, domain), 1) == iota((height, domain), 0) + member * height).astype(BF16)

    for copy in copies[3:]:
        copy.wait()
    n_items, n_req = items.shape[1], owners.shape[1]
    named = jnp.concatenate(
        [jnp.broadcast_to(items[...].astype(F32), (TILE, n_items)), jnp.zeros((TILE, domain - n_items), F32)], axis=1
    ).astype(BF16)
    source = owners[...] * pairs + wanted[...]
    hits = (source == iota((domain, n_req), 0)).astype(BF16)
    row, col = iota((TILE, n_req), 0), iota((TILE, n_req), 1)
    into = ((col // (n_req // pairs) == row // pairs) & (share[...] == row % pairs)).astype(BF16)
    extras = dot(into, hits, NT)
    terms, lines = pairs * pairs, 2 * pairs
    row = iota((TILE, domain), 0)
    line = (row - terms) % lines
    energy = jnp.zeros((TILE, domain), F32)
    for p in range(pairs):
        energy = jnp.where(line == p, virt[p : p + 1, :], energy)
        energy = jnp.where(line == pairs + p, pair[p], energy)
    high = energy.astype(BF16).astype(F32)
    middle = (energy - high).astype(BF16).astype(F32)
    low = energy - high - middle
    for k, part in enumerate((high, middle, low)):
        extras = jnp.where((row - terms) // lines == k, jnp.where(row >= terms, part, extras), extras)
    tail_out[:TILE, :] = extras.astype(BF16)
    lean_out[rows:, :] = named
    copies[0].wait()
    amp_half = amps[...].astype(BF16).reshape(rows, domain)
    lean_out[:rows, :] = amp_half
    copies[1].wait()
    half_out[...] = dot(chosen, block[0], NT).astype(BF16)
    tail_out[TILE:, :] = dot(mine, block[0], NT).astype(BF16)
    copies[2].wait()
    resid_out[...] = resid[...].astype(BF16).reshape(rows, domain)


def ordered(core, own, other):
    return jnp.where(core == 0, own, other), jnp.where(core == 0, other, own)


def partials(n_shared, items, pairs, own, far, far_tail, far_tail_c, half_own, *refs):
    y_refs, rest, (keep_out, give_out) = refs[: 2 * n_shared], refs[2 * n_shared : -2], refs[-2:]
    half_rows, domain = half_own.shape
    height = half_rows // 2
    rows = pairs * height
    group, _, core, family, half = place()
    near = [own] + list(y_refs[:n_shared])
    away = [far] + list(y_refs[n_shared:])
    x = [
        jnp.concatenate([piece[p * height : (p + 1) * height, :] for piece in side], axis=0)
        for side in (near, away)
        for p in range(pairs)
    ]
    x_all = jnp.concatenate(x, axis=0)
    deep = len(near) * height
    spread = (iota((rows, domain), 0) * items // rows == iota((rows, domain), 1)).astype(BF16)

    def names(piece):
        return dot(spread, jnp.broadcast_to(piece[rows : rows + TILE, :][:1], (half_rows, domain)), NT)

    named = [[names(piece) for piece in side] for side in (near, away)]
    ids = jnp.concatenate(
        [name[p * height : (p + 1) * height] for side in named for p in range(pairs) for name in side], axis=0
    ).astype(jnp.int32)

    def chosen(block, index):
        return jnp.where(ids == index, dot(x_all, block, NT), 0.0)

    def chosen_two(sofar, one, two, index, other):
        both = dot(x_all, jnp.concatenate([one, two], axis=0), NT)
        sofar = jnp.where(ids == index, both[:, :half_rows], sofar)
        return jnp.where(ids == other, both[:, half_rows:], sofar)

    if len(rest) > 1:
        count = len(rest) // 2
        mirror = jnp.concatenate(ordered(core, far_tail[TILE:, :], far_tail_c[TILE:, :]), axis=0)
        product = chosen_two(jnp.zeros(ids.shape, F32), half_own[...], mirror, group, group ^ half)
        for j in range(count):
            product = chosen_two(product, rest[j][...], rest[count + j][...], family ^ (j + 1), family ^ half ^ (j + 1))
    else:
        product = lax.fori_loop(
            0,
            rest[0].shape[0],
            lambda k, sofar: sofar + chosen(rest[0][k], k),
            jnp.zeros(ids.shape, F32),
        )
    product = product.astype(BF16)
    for p in range(pairs):
        both = [
            dot(product[k * deep : (k + 1) * deep], x[k], TN).astype(BF16) for k in (p, pairs + p)
        ]
        keep_out[p * half_rows : (p + 1) * half_rows, :], give_out[p * half_rows : (p + 1) * half_rows, :] = ordered(
            core, *both
        )


def joined(keep, given, out):
    out[...] = (keep[...].astype(F32) + given[...].astype(F32)).astype(BF16)


def spread_counts(own, far, swaps, half_rows, lanes):
    pairs = len(swaps)
    counts = jnp.concatenate([own[:TILE, :lanes], far[:TILE, :lanes]], axis=0)
    tall = 2 * pairs * pairs * half_rows
    term = iota((tall, 2 * TILE), 0) // half_rows
    which = term
    for p, swap in enumerate(swaps):
        which = jnp.where(term // pairs == pairs + p, TILE + swap * pairs + term % pairs, which)
    return dot((which == iota((tall, 2 * TILE), 1)).astype(BF16), counts).astype(BF16)


def weights(spread, source_group, pairs, half_rows):
    tall, lanes = spread.shape
    wide = pairs * half_rows
    same = iota((tall, wide), 0) % half_rows == iota((tall, wide), 1) % half_rows
    place_of = iota((lanes, wide), 0) == source_group * pairs + iota((lanes, wide), 1) // half_rows
    return jnp.where(same, dot(spread, place_of.astype(BF16)), 0.0).astype(BF16)


def lanes_of(pairs):
    return -(-lax.axis_size("pairs") * pairs // 128) * 128


def energies(packed, pairs):
    parts, lines, start = packed[:TILE, :].astype(F32), 2 * pairs, pairs * pairs
    energy = parts[start : start + lines]
    for k in (1, 2):
        energy += parts[start + k * lines : start + (k + 1) * lines]
    energy = jnp.concatenate([energy, jnp.zeros((8 - lines, energy.shape[1]), F32)], axis=0)
    return energy, energy.T


def inverse_of(energy, tall_energy, p, pairs):
    return 1.0 / (tall_energy[:, p : p + 1] + energy[p : p + 1] - energy[pairs + p : pairs + p + 1])


def near_factors(resid, own, inverse_out, base_out, held, sem):
    copy = pltpu.make_async_copy(resid, held, sem)
    copy.start()
    pairs, height, _ = resid.shape
    near = energies(own, pairs)
    for p in range(pairs):
        inverse_out[p] = inverse_of(*near, p, pairs)
    start = pl.multiple_of(lax.axis_index("ints") * height, height)
    copy.wait()
    base_out[...] = held[...] * inverse_out[:, pl.ds(start, height), :]


def factors(n_units, pairs, own, far, resid_far, swap, weights_out, inverse_out, bias_out, swap_out, held, sem):
    copy = pltpu.make_async_copy(swap, held, sem)
    copy.start()
    half_rows = weights_out.shape[0] // (2 * pairs * pairs)
    wide = pairs * half_rows
    group, _, _, family, half = place()
    height, domain = resid_far.shape[0] // pairs, resid_far.shape[1]
    spot = (iota((height, domain), 1) == iota((height, domain), 0) + lax.axis_index("ints") * height).astype(BF16)
    away = energies(far, pairs)
    away = [inverse_of(*away, p, pairs) for p in range(pairs)]
    copy.wait()
    swaps = [held[p] - (group ^ half) * pairs for p in range(pairs)]
    spread = spread_counts(own, far, swaps, half_rows, lanes_of(pairs))
    for k in range(n_units):
        weights_out[:, k * wide : (k + 1) * wide] = weights(spread, family ^ k, pairs, half_rows)
    for p in range(pairs):
        inverse_out[p] = functools.reduce(
            lambda kept, k: jnp.where(swaps[p] == k, away[k], kept), range(1, pairs), away[0]
        )
        parts = [resid_far[k * height : (k + 1) * height, :] for k in range(pairs)]
        part = functools.reduce(
            lambda kept, k: jnp.where(swaps[p] == k, parts[k], kept), range(1, pairs), parts[0]
        )
        bias_out[p] = dot(part, spot, TN) * inverse_out[p]
        swap_out[p] = jnp.full(swap_out.shape[1:], swaps[p], jnp.int32)


def cycle(n_sends, pairs, own, own_c, far, far_c, tail, far_tail, mix, inverse, inverse_far, bias, base, swap, *refs):
    units, (own_out, *sends), here = refs[: -n_sends - 2], refs[-n_sends - 2 : -1], refs[-1]
    height, domain = base.shape[1:]
    rows = pairs * height
    half_rows = 2 * height
    group, member, core, family, half = place()
    if len(units) > 1:
        mixed = dot(mix[...], jnp.concatenate([unit[...] for unit in units], axis=0))
    else:
        swaps = [swap[p, :1, :1] for p in range(pairs)]
        spread = spread_counts(tail, far_tail, swaps, half_rows, lanes_of(pairs))
        first = group - group % half
        mixed = lax.fori_loop(
            0,
            units[0].shape[0],
            lambda k, sofar: sofar
            + dot(weights(spread, (first + k) ^ (core * half), pairs, half_rows), units[0][k]),
            jnp.zeros((spread.shape[0], domain), F32),
        )
    mixed = mixed.astype(BF16)
    start = pl.ds(pl.multiple_of(member * height, height), height)

    def amps_of(mine, other):
        low, high = ordered(core, mine[:rows, :], other[:rows, :])
        return jnp.concatenate(
            [part[p * height : (p + 1) * height] for p in range(pairs) for part in (low, high)], axis=0
        )

    wide = pairs * half_rows
    near, away = amps_of(own, own_c), amps_of(far, far_c)
    for p in range(pairs):
        at = (pairs + p) * wide
        mirror = dot(away, mixed[at : at + wide], TN) * inverse_far[p] + bias[p]
        at = p * wide
        here[p] = dot(mixed[at : at + wide], near, TN) * inverse[p] + mirror
    own_out[...] = here[:, start, :] + base[...]
    for offset, send in enumerate(sends, 1):
        to = pl.multiple_of((member ^ offset) * height, height)
        send[...] = here[:, pl.ds(to, height), :].astype(BF16)


VM = pl.BlockSpec(memory_space=pltpu.VMEM)
HB = pl.BlockSpec(memory_space=pltpu.HBM)


def after(value, *others):
    return lax.optimization_barrier((value, *others))[0] if others else value


def stay(value):
    return pltpu.with_memory_space_constraint(value, pltpu.HBM)


def call(kernel, outs, in_specs, name, scratch=(), flops=0):
    return pl.pallas_call(
        kernel,
        out_shape=outs,
        in_specs=in_specs,
        out_specs=jax.tree.map(lambda _: VM, outs),
        scratch_shapes=scratch,
        name=name,
        cost_estimate=pl.CostEstimate(flops=flops, bytes_accessed=0, transcendentals=0) if flops else None,
        compiler_params=pltpu.CompilerParams(vmem_limit_bytes=48 * 1024 * 1024),
    )


def body(
    amps,
    resid_rest,
    int_blocks,
    virt_energy,
    pair_energy,
    item_block,
    share_owner,
    share_pair,
    share_amp,
    transpose_pair,
):
    n_pairs, n_ints = lax.axis_size("pairs"), lax.axis_size("ints")
    pairs, height, domain = amps.shape
    rows, half_rows, half = pairs * height, 2 * height, n_pairs // 2
    shape = jax.ShapeDtypeStruct
    operands = (
        amps,
        int_blocks,
        resid_rest,
        virt_energy,
        pair_energy,
        item_block.reshape(1, -1),
        share_owner.reshape(1, -1),
        share_pair.reshape(1, -1),
        share_amp.reshape(1, -1),
    )
    lean, half_own, tail, resid_half = call(
        prepare,
        [
            shape((rows + TILE, domain), BF16),
            shape((half_rows, domain), BF16),
            shape((TILE + height, domain), BF16),
            shape((rows, domain), BF16),
        ],
        [HB] * len(operands),
        "prepare",
        [(pltpu.SMEM if o is pair_energy else pltpu.VMEM)(o.shape, o.dtype) for o in operands]
        + [pltpu.SemaphoreType.DMA((len(operands),))],
    )(*map(stay, operands))
    inverse, base = call(
        near_factors,
        [shape((pairs, domain, domain), F32), shape((pairs, height, domain), F32)],
        [HB, VM],
        "near_factors",
        [pltpu.VMEM(resid_rest.shape, F32), pltpu.SemaphoreType.DMA],
        10**9,
    )(stay(resid_rest), tail)

    def across(value, *others):
        return exchange(after(value, *others), 0, CORE)

    far, far_tail = exchange(lean, half, 0), exchange(tail, half, 0)
    y_own = [exchange(lean, 0, k) for k in range(2, n_ints, 2)]
    blocks = [family_exchange(half_own, j) for j in range(1, half)] if n_pairs <= DIRECT else []
    y_far = [exchange(after(far, *y_own), 0, k) for k in range(2, n_ints, 2)]
    far_tail_c = across(far_tail)
    if n_pairs <= DIRECT:
        blocks += [across(block) for block in blocks]
    else:
        blocks = [lax.all_gather(half_own, "pairs", axis=0, tiled=False)]
    keep, give = call(
        functools.partial(partials, len(y_own), item_block.shape[0], pairs),
        [shape((pairs * half_rows, domain), BF16)] * 2,
        [VM] * (5 + len(y_own) + len(y_far) + len(blocks)),
        "partials",
    )(lean, far, far_tail, far_tail_c, half_own, *y_own, *y_far, *blocks)
    inter = call(joined, shape((pairs * half_rows, domain), BF16), [VM] * 2, "joined")(keep, across(give))
    own_c, far_c = across(lean), across(far)
    if n_pairs <= DIRECT:
        units = [inter] + [exchange(inter, j, 0) for j in range(1, half)]
    else:
        every = lax.all_gather(inter, "pairs", axis=0, tiled=False)
        first = lax.axis_index("pairs") // half * half
        units = [lax.dynamic_slice_in_dim(every, first, half, 0)]
    resid_far = exchange(resid_half, half, 0)
    n_units = len(units)
    mix, inverse_far, bias, swap = call(
        functools.partial(factors, n_units if n_units > 1 else 0, pairs),
        [
            shape((2 * pairs * pairs * half_rows, n_units * pairs * half_rows), BF16),
            shape((pairs, domain, domain), F32),
            shape((pairs, domain, domain), F32),
            shape((pairs, 8, 128), jnp.int32),
        ],
        [VM, VM, VM, HB],
        "factors",
        [pltpu.SMEM(transpose_pair.shape, jnp.int32), pltpu.SemaphoreType.DMA],
    )(tail, far_tail, resid_far, stay(transpose_pair))
    mine, *sends = call(
        functools.partial(cycle, n_ints - 1, pairs),
        [shape((pairs, height, domain), F32)] + [shape((pairs, height, domain), BF16)] * (n_ints - 1),
        [VM] * (12 + n_units),
        "cycle",
        [pltpu.VMEM((pairs, domain, domain), F32)],
    )(lean, own_c, far, far_c, tail, far_tail, mix, inverse, inverse_far, bias, base, swap, *units)
    for offset in [*range(2, n_ints), 1]:
        mine = mine + exchange(sends[offset - 1], 0, offset).astype(F32)
    return -0.5 * mine


def solution(mesh):
    placed = (
        P("pairs", "ints", None),
        P("pairs", "ints", None),
        P("pairs", None, None),
        P("pairs", None),
        P("pairs"),
        P(("pairs", "ints"), None),
        P("pairs", None),
        P("pairs", None),
        P("pairs", None),
        P("pairs"),
    )
    return jax.shard_map(
        body, mesh=mesh, in_specs=placed, out_specs=P("pairs", "ints", None), check_vma=False
    )
```

```python
import functools

import jax
import jax.numpy as jnp
from jax import lax
from jax.experimental import pallas as pl
from jax.experimental.pallas import tpu as pltpu
from jax.sharding import PartitionSpec as P

F32, BF16 = jnp.float32, jnp.bfloat16
DIRECT = 16
CORE = 1
NT = (((1,), (1,)), ((), ()))
TN = (((0,), (0,)), ((), ()))
TILE = 16


def dot(a, b, dims=(((1,), (0,)), ((), ()))):
    return lax.dot_general(a, b, dims, preferred_element_type=F32)


def iota(shape, dim):
    return lax.broadcasted_iota(jnp.int32, shape, dim)


def exchange(value, pair_offset, int_offset):
    n_pairs, n_ints = lax.axis_size("pairs"), lax.axis_size("ints")
    route = [
        (p * n_ints + q, (p ^ pair_offset) * n_ints + (q ^ int_offset)) for p in range(n_pairs) for q in range(n_ints)
    ]
    return lax.ppermute(value, ("pairs", "ints"), route)


def family_exchange(value, offset):
    n_pairs, n_ints = lax.axis_size("pairs"), lax.axis_size("ints")
    half = n_pairs // 2
    route = [
        (p * n_ints + q, (p ^ offset ^ (q % 2 * half)) * n_ints + q) for p in range(n_pairs) for q in range(n_ints)
    ]
    return lax.ppermute(value, ("pairs", "ints"), route)


def place():
    group, member, n_pairs = lax.axis_index("pairs"), lax.axis_index("ints"), lax.axis_size("pairs")
    core = member % 2
    return group, member, core, group ^ (core * (n_pairs // 2)), n_pairs // 2


def prepare(
    amps, block, resid, virt, pair, items, owners, wanted, share, lean_out, half_out, tail_out, resid_out, *scratch
):
    hbm = (amps, block, resid, virt, pair, items, owners, wanted, share)
    held, sems = scratch[:-1], scratch[-1]
    copies = [pltpu.make_async_copy(src, dst, sems.at[i]) for i, (src, dst) in enumerate(zip(hbm, held))]
    for copy in copies:
        copy.start()
    amps, block, resid, virt, pair, items, owners, wanted, share = held
    pairs, height, domain = amps.shape
    rows = pairs * height
    member = lax.axis_index("ints")
    half_rows = half_out.shape[0]
    half_start = member // 2 * half_rows
    chosen = (iota((half_rows, domain), 1) == iota((half_rows, domain), 0) + half_start).astype(BF16)
    mine = (iota((height, domain), 1) == iota((height, domain), 0) + member * height).astype(BF16)

    for copy in copies[3:]:
        copy.wait()
    n_items, n_req = items.shape[1], owners.shape[1]
    named = jnp.concatenate(
        [jnp.broadcast_to(items[...].astype(F32), (TILE, n_items)), jnp.zeros((TILE, domain - n_items), F32)], axis=1
    ).astype(BF16)
    source = owners[...] * pairs + wanted[...]
    hits = (source == iota((domain, n_req), 0)).astype(BF16)
    row, col = iota((TILE, n_req), 0), iota((TILE, n_req), 1)
    into = ((col // (n_req // pairs) == row // pairs) & (share[...] == row % pairs)).astype(BF16)
    extras = dot(into, hits, NT)
    terms, lines = pairs * pairs, 2 * pairs
    row = iota((TILE, domain), 0)
    line = (row - terms) % lines
    energy = jnp.zeros((TILE, domain), F32)
    for p in range(pairs):
        energy = jnp.where(line == p, virt[p : p + 1, :], energy)
        energy = jnp.where(line == pairs + p, pair[p], energy)
    high = energy.astype(BF16).astype(F32)
    middle = (energy - high).astype(BF16).astype(F32)
    low = energy - high - middle
    for k, part in enumerate((high, middle, low)):
        extras = jnp.where((row - terms) // lines == k, jnp.where(row >= terms, part, extras), extras)
    tail_out[:TILE, :] = extras.astype(BF16)
    lean_out[rows:, :] = named
    copies[0].wait()
    amp_half = amps[...].astype(BF16).reshape(rows, domain)
    lean_out[:rows, :] = amp_half
    copies[1].wait()
    half_out[...] = dot(chosen, block[0], NT).astype(BF16)
    tail_out[TILE:, :] = dot(mine, block[0], NT).astype(BF16)
    copies[2].wait()
    resid_out[...] = resid[...].astype(BF16).reshape(rows, domain)


def ordered(core, own, other):
    return jnp.where(core == 0, own, other), jnp.where(core == 0, other, own)


def partials(n_shared, items, pairs, own, far, far_tail, far_tail_c, half_own, *refs):
    y_refs, rest, (keep_out, give_out) = refs[: 2 * n_shared], refs[2 * n_shared : -2], refs[-2:]
    half_rows, domain = half_own.shape
    height = half_rows // 2
    rows = pairs * height
    group, _, core, family, half = place()
    near = [own] + list(y_refs[:n_shared])
    away = [far] + list(y_refs[n_shared:])
    x = [
        jnp.concatenate([piece[p * height : (p + 1) * height, :] for piece in side], axis=0)
        for side in (near, away)
        for p in range(pairs)
    ]
    x_all = jnp.concatenate(x, axis=0)
    deep = len(near) * height
    spread = (iota((rows, domain), 0) * items // rows == iota((rows, domain), 1)).astype(BF16)

    def names(piece):
        return dot(spread, jnp.broadcast_to(piece[rows : rows + TILE, :][:1], (half_rows, domain)), NT)

    named = [[names(piece) for piece in side] for side in (near, away)]
    ids = jnp.concatenate(
        [name[p * height : (p + 1) * height] for side in named for p in range(pairs) for name in side], axis=0
    ).astype(jnp.int32)

    def chosen(block, index):
        return jnp.where(ids == index, dot(x_all, block, NT), 0.0)

    def chosen_two(sofar, one, two, index, other):
        both = dot(x_all, jnp.concatenate([one, two], axis=0), NT)
        sofar = jnp.where(ids == index, both[:, :half_rows], sofar)
        return jnp.where(ids == other, both[:, half_rows:], sofar)

    if len(rest) > 1:
        count = len(rest) // 2
        mirror = jnp.concatenate(ordered(core, far_tail[TILE:, :], far_tail_c[TILE:, :]), axis=0)
        product = chosen_two(jnp.zeros(ids.shape, F32), half_own[...], mirror, group, group ^ half)
        for j in range(count):
            product = chosen_two(product, rest[j][...], rest[count + j][...], family ^ (j + 1), family ^ half ^ (j + 1))
    else:
        product = lax.fori_loop(
            0,
            rest[0].shape[0],
            lambda k, sofar: sofar + chosen(rest[0][k], k),
            jnp.zeros(ids.shape, F32),
        )
    product = product.astype(BF16)
    for p in range(pairs):
        both = [
            dot(product[k * deep : (k + 1) * deep], x[k], TN).astype(BF16) for k in (p, pairs + p)
        ]
        keep_out[p * half_rows : (p + 1) * half_rows, :], give_out[p * half_rows : (p + 1) * half_rows, :] = ordered(
            core, *both
        )


def joined(keep, given, out):
    out[...] = (keep[...].astype(F32) + given[...].astype(F32)).astype(BF16)


def spread_counts(own, far, swaps, half_rows, lanes):
    pairs = len(swaps)
    counts = jnp.concatenate([own[:TILE, :lanes], far[:TILE, :lanes]], axis=0)
    tall = 2 * pairs * pairs * half_rows
    term = iota((tall, 2 * TILE), 0) // half_rows
    which = term
    for p, swap in enumerate(swaps):
        which = jnp.where(term // pairs == pairs + p, TILE + swap * pairs + term % pairs, which)
    return dot((which == iota((tall, 2 * TILE), 1)).astype(BF16), counts).astype(BF16)


def shares(spread, source_group, at, pairs, half_rows, flipped):
    wide, lanes = pairs * half_rows, spread.shape[1]
    picked = (iota((wide, lanes), 1) == source_group * pairs + iota((wide, lanes), 0) // half_rows).astype(BF16)
    part = spread[at * wide : (at + 1) * wide]
    same = iota((wide, wide), 0) % half_rows == iota((wide, wide), 1) % half_rows
    return jnp.where(same, dot(part, picked, NT) if flipped else dot(picked, part, NT), 0.0).astype(BF16)


def rows_of(core, mine, other, pairs):
    rows = mine.shape[0] - TILE
    height = rows // pairs
    low, high = ordered(core, mine[:rows, :], other[:rows, :])
    return jnp.concatenate(
        [part[p * height : (p + 1) * height] for p in range(pairs) for part in (low, high)], axis=0
    )


def mixed_rows(spread, source_group, near, away, pairs, half_rows):
    z = [dot(shares(spread, source_group, p, pairs, half_rows, False), near) for p in range(pairs)]
    zt = [dot(away, shares(spread, source_group, pairs + p, pairs, half_rows, True), TN) for p in range(pairs)]
    return jnp.concatenate(z, axis=1).astype(BF16), jnp.concatenate(zt, axis=0).astype(BF16)


def lanes_of(pairs):
    return -(-lax.axis_size("pairs") * pairs // 128) * 128


def energies(packed, pairs):
    parts, lines, start = packed[:TILE, :].astype(F32), 2 * pairs, pairs * pairs
    energy = parts[start : start + lines]
    for k in (1, 2):
        energy += parts[start + k * lines : start + (k + 1) * lines]
    energy = jnp.concatenate([energy, jnp.zeros((8 - lines, energy.shape[1]), F32)], axis=0)
    return energy, energy.T


def inverse_of(energy, tall_energy, p, pairs):
    return 1.0 / (tall_energy[:, p : p + 1] + energy[p : p + 1] - energy[pairs + p : pairs + p + 1])


def near_factors(resid, own, inverse_out, base_out, held, sem):
    copy = pltpu.make_async_copy(resid, held, sem)
    copy.start()
    pairs, height, _ = resid.shape
    near = energies(own, pairs)
    for p in range(pairs):
        inverse_out[p] = inverse_of(*near, p, pairs)
    start = pl.multiple_of(lax.axis_index("ints") * height, height)
    copy.wait()
    base_out[...] = held[...] * inverse_out[:, pl.ds(start, height), :]


def factors(
    n_units, pairs, own, own_c, far, far_c, tail, far_tail, resid_far, swap, z_out, zt_out, inverse_out, bias_out, swap_out, held, sem
):
    copy = pltpu.make_async_copy(swap, held, sem)
    copy.start()
    group, _, core, family, half = place()
    height, domain = resid_far.shape[0] // pairs, resid_far.shape[1]
    half_rows = 2 * height
    wide = pairs * half_rows
    spot = (iota((height, domain), 1) == iota((height, domain), 0) + lax.axis_index("ints") * height).astype(BF16)
    away = energies(far_tail, pairs)
    away = [inverse_of(*away, p, pairs) for p in range(pairs)]
    copy.wait()
    swaps = [held[p] - (group ^ half) * pairs for p in range(pairs)]
    if n_units:
        spread = spread_counts(tail, far_tail, swaps, half_rows, lanes_of(pairs))
        near_rows, away_rows = rows_of(core, own, own_c, pairs), rows_of(core, far, far_c, pairs)
    for k in range(n_units):
        z, zt = mixed_rows(spread, family ^ k, near_rows, away_rows, pairs, half_rows)
        z_out[k * wide : (k + 1) * wide, :] = z
        zt_out[:, k * wide : (k + 1) * wide] = zt
    for p in range(pairs):
        inverse_out[p] = functools.reduce(
            lambda kept, k: jnp.where(swaps[p] == k, away[k], kept), range(1, pairs), away[0]
        )
        parts = [resid_far[k * height : (k + 1) * height, :] for k in range(pairs)]
        part = functools.reduce(
            lambda kept, k: jnp.where(swaps[p] == k, parts[k], kept), range(1, pairs), parts[0]
        )
        bias_out[p] = dot(part, spot, TN) * inverse_out[p]
        swap_out[p] = jnp.full(swap_out.shape[1:], swaps[p], jnp.int32)


def summed(units, starts, z, zt):
    both = jnp.concatenate([unit[...] for unit in units], axis=0)
    wide = units[0].shape[0]
    z_part = jnp.concatenate([z[k * wide : (k + 1) * wide, :] for k in starts], axis=0)
    zt_part = jnp.concatenate([zt[:, k * wide : (k + 1) * wide] for k in starts], axis=1)
    return dot(both, z_part, TN), dot(zt_part, both)


def cycle_first(starts, pairs, own, own_c, far, far_c, tail, far_tail, z, zt, swap, *refs):
    units, near_out, away_out = refs[:-2], refs[-2], refs[-1]
    if starts:
        near_out[...], away_out[...] = summed(units, starts, z, zt)
        return
    half_rows = units[0].shape[1] // pairs
    group, _, core, _, half = place()
    spread = spread_counts(tail, far_tail, [swap[p, :1, :1] for p in range(pairs)], half_rows, lanes_of(pairs))
    near_rows, away_rows = rows_of(core, own, own_c, pairs), rows_of(core, far, far_c, pairs)
    first = group - group % half
    near_out[...], away_out[...] = jnp.zeros(near_out.shape, F32), jnp.zeros(away_out.shape, F32)

    def step(k, none):
        part, part_t = mixed_rows(spread, (first + k) ^ (core * half), near_rows, away_rows, pairs, half_rows)
        near_out[...] += dot(units[0][k], part, TN)
        away_out[...] += dot(part_t, units[0][k])
        return none

    lax.fori_loop(0, units[0].shape[0], step, 0)


def cycle_last(n_sends, starts, z, zt, near, away, inverse, inverse_far, bias, base, *refs):
    units, (own_out, *sends), here = refs[: -n_sends - 2], refs[-n_sends - 2 : -1], refs[-1]
    pairs, height, domain = base.shape
    member = lax.axis_index("ints")
    near, away = near[...], away[...]
    if units:
        more, more_away = summed(units, starts, z, zt)
        near, away = near + more, away + more_away
    for p in range(pairs):
        part = slice(p * domain, (p + 1) * domain)
        here[p] = near[:, part] * inverse[p] + (away[part] * inverse_far[p] + bias[p])
    start = pl.ds(pl.multiple_of(member * height, height), height)
    own_out[...] = here[:, start, :] + base[...]
    for offset, send in enumerate(sends, 1):
        to = pl.multiple_of((member ^ offset) * height, height)
        send[...] = here[:, pl.ds(to, height), :].astype(BF16)


VM = pl.BlockSpec(memory_space=pltpu.VMEM)
HB = pl.BlockSpec(memory_space=pltpu.HBM)


def after(value, *others):
    return lax.optimization_barrier((value, *others))[0] if others else value


def stay(value):
    return pltpu.with_memory_space_constraint(value, pltpu.HBM)


def call(kernel, outs, in_specs, name, scratch=(), flops=0):
    return pl.pallas_call(
        kernel,
        out_shape=outs,
        in_specs=in_specs,
        out_specs=jax.tree.map(lambda _: VM, outs),
        scratch_shapes=scratch,
        name=name,
        cost_estimate=pl.CostEstimate(flops=flops, bytes_accessed=0, transcendentals=0) if flops else None,
        compiler_params=pltpu.CompilerParams(vmem_limit_bytes=48 * 1024 * 1024),
    )


def body(
    amps,
    resid_rest,
    int_blocks,
    virt_energy,
    pair_energy,
    item_block,
    share_owner,
    share_pair,
    share_amp,
    transpose_pair,
):
    n_pairs, n_ints = lax.axis_size("pairs"), lax.axis_size("ints")
    pairs, height, domain = amps.shape
    rows, half_rows, half = pairs * height, 2 * height, n_pairs // 2
    shape = jax.ShapeDtypeStruct
    operands = (
        amps,
        int_blocks,
        resid_rest,
        virt_energy,
        pair_energy,
        item_block.reshape(1, -1),
        share_owner.reshape(1, -1),
        share_pair.reshape(1, -1),
        share_amp.reshape(1, -1),
    )
    lean, half_own, tail, resid_half = call(
        prepare,
        [
            shape((rows + TILE, domain), BF16),
            shape((half_rows, domain), BF16),
            shape((TILE + height, domain), BF16),
            shape((rows, domain), BF16),
        ],
        [HB] * len(operands),
        "prepare",
        [(pltpu.SMEM if o is pair_energy else pltpu.VMEM)(o.shape, o.dtype) for o in operands]
        + [pltpu.SemaphoreType.DMA((len(operands),))],
    )(*map(stay, operands))
    inverse, base = call(
        near_factors,
        [shape((pairs, domain, domain), F32), shape((pairs, height, domain), F32)],
        [HB, VM],
        "near_factors",
        [pltpu.VMEM(resid_rest.shape, F32), pltpu.SemaphoreType.DMA],
        10**9,
    )(stay(resid_rest), tail)

    def across(value, *others):
        return exchange(after(value, *others), 0, CORE)

    far, far_tail = exchange(lean, half, 0), exchange(tail, half, 0)
    y_own = [exchange(lean, 0, k) for k in range(2, n_ints, 2)]
    blocks = [family_exchange(half_own, j) for j in range(1, half)] if n_pairs <= DIRECT else []
    y_far = [exchange(after(far, *y_own), 0, k) for k in range(2, n_ints, 2)]
    far_tail_c = across(far_tail)
    if n_pairs <= DIRECT:
        blocks += [across(block) for block in blocks]
    else:
        blocks = [lax.all_gather(half_own, "pairs", axis=0, tiled=False)]
    keep, give = call(
        functools.partial(partials, len(y_own), item_block.shape[0], pairs),
        [shape((pairs * half_rows, domain), BF16)] * 2,
        [VM] * (5 + len(y_own) + len(y_far) + len(blocks)),
        "partials",
    )(lean, far, far_tail, far_tail_c, half_own, *y_own, *y_far, *blocks)
    inter = call(joined, shape((pairs * half_rows, domain), BF16), [VM] * 2, "joined")(keep, across(give))
    own_c, far_c = across(lean), across(far)
    if n_pairs <= DIRECT:
        units = [inter] + [exchange(inter, j, 0) for j in range(1, half)]
    else:
        every = lax.all_gather(inter, "pairs", axis=0, tiled=False)
        first = lax.axis_index("pairs") // half * half
        units = [lax.dynamic_slice_in_dim(every, first, half, 0)]
    resid_far = exchange(resid_half, half, 0)
    n_units = len(units)
    wide, planned = pairs * half_rows, n_units if n_units > 1 else 0
    z, zt, inverse_far, bias, swap = call(
        functools.partial(factors, planned, pairs),
        [
            shape((n_units * wide, pairs * domain), BF16),
            shape((pairs * domain, n_units * wide), BF16),
            shape((pairs, domain, domain), F32),
            shape((pairs, domain, domain), F32),
            shape((pairs, 8, 128), jnp.int32),
        ],
        [VM] * 7 + [HB],
        "factors",
        [pltpu.SMEM(transpose_pair.shape, jnp.int32), pltpu.SemaphoreType.DMA],
    )(lean, own_c, far, far_c, tail, far_tail, resid_far, stay(transpose_pair))
    early = [0, planned - 1] if planned else []
    late = [k for k in range(planned) if k not in early]
    first_units = [units[k] for k in early] or units
    near, away = call(
        functools.partial(cycle_first, early, pairs),
        [shape((domain, pairs * domain), F32), shape((pairs * domain, domain), F32)],
        [VM] * (9 + len(first_units)),
        "cycle_first",
    )(lean, own_c, far, far_c, tail, far_tail, z, zt, swap, *first_units)
    mine, *sends = call(
        functools.partial(cycle_last, n_ints - 1, late),
        [shape((pairs, height, domain), F32)] + [shape((pairs, height, domain), BF16)] * (n_ints - 1),
        [VM] * (8 + len(late)),
        "cycle_last",
        [pltpu.VMEM((pairs, domain, domain), F32)],
    )(z, zt, near, away, inverse, inverse_far, bias, base, *[units[k] for k in late])
    for offset in [*range(2, n_ints), 1]:
        mine = mine + exchange(sends[offset - 1], 0, offset).astype(F32)
    return -0.5 * mine


def solution(mesh):
    placed = (
        P("pairs", "ints", None),
        P("pairs", "ints", None),
        P("pairs", None, None),
        P("pairs", None),
        P("pairs"),
        P(("pairs", "ints"), None),
        P("pairs", None),
        P("pairs", None),
        P("pairs", None),
        P("pairs"),
    )
    return jax.shard_map(
        body, mesh=mesh, in_specs=placed, out_specs=P("pairs", "ints", None), check_vma=False
    )
```

```python
import functools

import jax
import jax.numpy as jnp
from jax import lax
from jax.experimental import pallas as pl
from jax.experimental.pallas import tpu as pltpu
from jax.sharding import PartitionSpec as P

F32, BF16 = jnp.float32, jnp.bfloat16
DIRECT = 16
CORE = 1
NT = (((1,), (1,)), ((), ()))
TN = (((0,), (0,)), ((), ()))
TILE = 16


def dot(a, b, dims=(((1,), (0,)), ((), ()))):
    return lax.dot_general(a, b, dims, preferred_element_type=F32)


def iota(shape, dim):
    return lax.broadcasted_iota(jnp.int32, shape, dim)


def exchange(value, pair_offset, int_offset):
    n_pairs, n_ints = lax.axis_size("pairs"), lax.axis_size("ints")
    route = [
        (p * n_ints + q, (p ^ pair_offset) * n_ints + (q ^ int_offset)) for p in range(n_pairs) for q in range(n_ints)
    ]
    return lax.ppermute(value, ("pairs", "ints"), route)


def family_exchange(value, offset):
    n_pairs, n_ints = lax.axis_size("pairs"), lax.axis_size("ints")
    half = n_pairs // 2
    route = [
        (p * n_ints + q, (p ^ offset ^ (q % 2 * half)) * n_ints + q) for p in range(n_pairs) for q in range(n_ints)
    ]
    return lax.ppermute(value, ("pairs", "ints"), route)


def place():
    group, member, n_pairs = lax.axis_index("pairs"), lax.axis_index("ints"), lax.axis_size("pairs")
    core = member % 2
    return group, member, core, group ^ (core * (n_pairs // 2)), n_pairs // 2


def prepare(
    amps, block, resid, virt, pair, items, owners, wanted, share, lean_out, half_out, tail_out, resid_out, *scratch
):
    hbm = (amps, block, resid, virt, pair, items, owners, wanted, share)
    held, sems = scratch[:-1], scratch[-1]
    copies = [pltpu.make_async_copy(src, dst, sems.at[i]) for i, (src, dst) in enumerate(zip(hbm, held))]
    for copy in copies:
        copy.start()
    amps, block, resid, virt, pair, items, owners, wanted, share = held
    pairs, height, domain = amps.shape
    rows = pairs * height
    member = lax.axis_index("ints")
    half_rows = half_out.shape[0]
    half_start = member // 2 * half_rows
    chosen = (iota((half_rows, domain), 1) == iota((half_rows, domain), 0) + half_start).astype(BF16)
    mine = (iota((height, domain), 1) == iota((height, domain), 0) + member * height).astype(BF16)

    for copy in copies[3:]:
        copy.wait()
    n_items, n_req = items.shape[1], owners.shape[1]
    named = jnp.concatenate(
        [jnp.broadcast_to(items[...].astype(F32), (TILE, n_items)), jnp.zeros((TILE, domain - n_items), F32)], axis=1
    ).astype(BF16)
    source = owners[...] * pairs + wanted[...]
    hits = (source == iota((domain, n_req), 0)).astype(BF16)
    row, col = iota((TILE, n_req), 0), iota((TILE, n_req), 1)
    into = ((col // (n_req // pairs) == row // pairs) & (share[...] == row % pairs)).astype(BF16)
    extras = dot(into, hits, NT)
    terms, lines = pairs * pairs, 2 * pairs
    row = iota((TILE, domain), 0)
    line = (row - terms) % lines
    energy = jnp.zeros((TILE, domain), F32)
    for p in range(pairs):
        energy = jnp.where(line == p, virt[p : p + 1, :], energy)
        energy = jnp.where(line == pairs + p, pair[p], energy)
    high = energy.astype(BF16).astype(F32)
    middle = (energy - high).astype(BF16).astype(F32)
    low = energy - high - middle
    for k, part in enumerate((high, middle, low)):
        extras = jnp.where((row - terms) // lines == k, jnp.where(row >= terms, part, extras), extras)
    tail_out[:TILE, :] = extras.astype(BF16)
    lean_out[rows:, :] = named
    copies[0].wait()
    amp_half = amps[...].astype(BF16).reshape(rows, domain)
    lean_out[:rows, :] = amp_half
    copies[1].wait()
    half_out[...] = dot(chosen, block[0], NT).astype(BF16)
    tail_out[TILE:, :] = dot(mine, block[0], NT).astype(BF16)
    copies[2].wait()
    resid_out[...] = resid[...].astype(BF16).reshape(rows, domain)


def ordered(core, own, other):
    return jnp.where(core == 0, own, other), jnp.where(core == 0, other, own)


def products(n_shared, items, pairs, own, far, half_own, *refs):
    y_refs, rest, (product_out, ids_out) = refs[: 2 * n_shared], refs[2 * n_shared : -2], refs[-2:]
    half_rows, domain = half_own.shape
    height = half_rows // 2
    rows = pairs * height
    group, _, core, family, half = place()
    near = [own] + list(y_refs[:n_shared])
    away = [far] + list(y_refs[n_shared:])
    x = [
        jnp.concatenate([piece[p * height : (p + 1) * height, :] for piece in side], axis=0)
        for side in (near, away)
        for p in range(pairs)
    ]
    x_all = jnp.concatenate(x, axis=0)
    deep = len(near) * height
    spread = (iota((rows, domain), 0) * items // rows == iota((rows, domain), 1)).astype(BF16)

    def names(piece):
        return dot(spread, jnp.broadcast_to(piece[rows : rows + TILE, :][:1], (half_rows, domain)), NT)

    named = [[names(piece) for piece in side] for side in (near, away)]
    ids = jnp.concatenate(
        [name[p * height : (p + 1) * height] for side in named for p in range(pairs) for name in side], axis=0
    ).astype(jnp.int32)

    def chosen(block, index):
        return jnp.where(ids == index, dot(x_all, block, NT), 0.0)

    def chosen_two(sofar, one, two, index, other):
        both = dot(x_all, jnp.concatenate([one, two], axis=0), NT)
        sofar = jnp.where(ids == index, both[:, :half_rows], sofar)
        return jnp.where(ids == other, both[:, half_rows:], sofar)

    if len(rest) > 1:
        count = len(rest) // 2
        product = chosen(half_own[...], group)
        for j in range(count):
            product = chosen_two(product, rest[j][...], rest[count + j][...], family ^ (j + 1), family ^ half ^ (j + 1))
    else:
        product = lax.fori_loop(
            0,
            rest[0].shape[0],
            lambda k, sofar: sofar + chosen(rest[0][k], k),
            jnp.zeros(ids.shape, F32),
        )
    product_out[...] = product
    ids_out[...] = ids


def partials(n_shared, pairs, direct, own, far, far_tail, far_tail_c, product, ids, *refs):
    y_refs, (keep_out, give_out) = refs[: 2 * n_shared], refs[2 * n_shared :]
    half_rows, domain = ids.shape[1], own.shape[1]
    height = half_rows // 2
    group, _, core, family, half = place()
    near = [own] + list(y_refs[:n_shared])
    away = [far] + list(y_refs[n_shared:])
    x = [
        jnp.concatenate([piece[p * height : (p + 1) * height, :] for piece in side], axis=0)
        for side in (near, away)
        for p in range(pairs)
    ]
    x_all = jnp.concatenate(x, axis=0)
    deep = len(near) * height
    product = product[...]
    if direct:
        mirror = jnp.concatenate(ordered(core, far_tail[TILE:, :], far_tail_c[TILE:, :]), axis=0)
        product = jnp.where(ids[...] == (group ^ half), dot(x_all, mirror, NT), product)
    product = product.astype(BF16)
    for p in range(pairs):
        both = [
            dot(product[k * deep : (k + 1) * deep], x[k], TN).astype(BF16) for k in (p, pairs + p)
        ]
        keep_out[p * half_rows : (p + 1) * half_rows, :], give_out[p * half_rows : (p + 1) * half_rows, :] = ordered(
            core, *both
        )


def joined(keep, given, out):
    out[...] = (keep[...].astype(F32) + given[...].astype(F32)).astype(BF16)


def spread_counts(own, far, swaps, half_rows, lanes):
    pairs = len(swaps)
    counts = jnp.concatenate([own[:TILE, :lanes], far[:TILE, :lanes]], axis=0)
    tall = 2 * pairs * pairs * half_rows
    term = iota((tall, 2 * TILE), 0) // half_rows
    which = term
    for p, swap in enumerate(swaps):
        which = jnp.where(term // pairs == pairs + p, TILE + swap * pairs + term % pairs, which)
    return dot((which == iota((tall, 2 * TILE), 1)).astype(BF16), counts).astype(BF16)


def shares(spread, source_group, at, pairs, half_rows, flipped):
    wide, lanes = pairs * half_rows, spread.shape[1]
    picked = (iota((wide, lanes), 1) == source_group * pairs + iota((wide, lanes), 0) // half_rows).astype(BF16)
    part = spread[at * wide : (at + 1) * wide]
    same = iota((wide, wide), 0) % half_rows == iota((wide, wide), 1) % half_rows
    return jnp.where(same, dot(part, picked, NT) if flipped else dot(picked, part, NT), 0.0).astype(BF16)


def rows_of(core, mine, other, pairs):
    rows = mine.shape[0] - TILE
    height = rows // pairs
    low, high = ordered(core, mine[:rows, :], other[:rows, :])
    return jnp.concatenate(
        [part[p * height : (p + 1) * height] for p in range(pairs) for part in (low, high)], axis=0
    )


def mixed_rows(spread, source_group, near, away, pairs, half_rows):
    z = [dot(shares(spread, source_group, p, pairs, half_rows, False), near) for p in range(pairs)]
    zt = [dot(away, shares(spread, source_group, pairs + p, pairs, half_rows, True), TN) for p in range(pairs)]
    return jnp.concatenate(z, axis=1).astype(BF16), jnp.concatenate(zt, axis=0).astype(BF16)


def lanes_of(pairs):
    return -(-lax.axis_size("pairs") * pairs // 128) * 128


def energies(packed, pairs):
    parts, lines, start = packed[:TILE, :].astype(F32), 2 * pairs, pairs * pairs
    energy = parts[start : start + lines]
    for k in (1, 2):
        energy += parts[start + k * lines : start + (k + 1) * lines]
    energy = jnp.concatenate([energy, jnp.zeros((8 - lines, energy.shape[1]), F32)], axis=0)
    return energy, energy.T


def inverse_of(energy, tall_energy, p, pairs):
    return 1.0 / (tall_energy[:, p : p + 1] + energy[p : p + 1] - energy[pairs + p : pairs + p + 1])


def near_factors(resid, own, inverse_out, base_out, held, sem):
    copy = pltpu.make_async_copy(resid, held, sem)
    copy.start()
    pairs, height, _ = resid.shape
    near = energies(own, pairs)
    for p in range(pairs):
        inverse_out[p] = inverse_of(*near, p, pairs)
    start = pl.multiple_of(lax.axis_index("ints") * height, height)
    copy.wait()
    base_out[...] = held[...] * inverse_out[:, pl.ds(start, height), :]


def factors(
    n_units, pairs, own, own_c, far, far_c, tail, far_tail, resid_far, swap, z_out, zt_out, inverse_out, bias_out, swap_out, held, sem
):
    copy = pltpu.make_async_copy(swap, held, sem)
    copy.start()
    group, _, core, family, half = place()
    height, domain = resid_far.shape[0] // pairs, resid_far.shape[1]
    half_rows = 2 * height
    wide = pairs * half_rows
    spot = (iota((height, domain), 1) == iota((height, domain), 0) + lax.axis_index("ints") * height).astype(BF16)
    away = energies(far_tail, pairs)
    away = [inverse_of(*away, p, pairs) for p in range(pairs)]
    copy.wait()
    swaps = [held[p] - (group ^ half) * pairs for p in range(pairs)]
    if n_units:
        spread = spread_counts(tail, far_tail, swaps, half_rows, lanes_of(pairs))
        near_rows, away_rows = rows_of(core, own, own_c, pairs), rows_of(core, far, far_c, pairs)
    for k in range(n_units):
        z, zt = mixed_rows(spread, family ^ k, near_rows, away_rows, pairs, half_rows)
        z_out[k * wide : (k + 1) * wide, :] = z
        zt_out[:, k * wide : (k + 1) * wide] = zt
    for p in range(pairs):
        inverse_out[p] = functools.reduce(
            lambda kept, k: jnp.where(swaps[p] == k, away[k], kept), range(1, pairs), away[0]
        )
        parts = [resid_far[k * height : (k + 1) * height, :] for k in range(pairs)]
        part = functools.reduce(
            lambda kept, k: jnp.where(swaps[p] == k, parts[k], kept), range(1, pairs), parts[0]
        )
        bias_out[p] = dot(part, spot, TN) * inverse_out[p]
        swap_out[p] = jnp.full(swap_out.shape[1:], swaps[p], jnp.int32)


def summed(units, starts, z, zt):
    both = jnp.concatenate([unit[...] for unit in units], axis=0)
    wide = units[0].shape[0]
    z_part = jnp.concatenate([z[k * wide : (k + 1) * wide, :] for k in starts], axis=0)
    zt_part = jnp.concatenate([zt[:, k * wide : (k + 1) * wide] for k in starts], axis=1)
    return dot(both, z_part, TN), dot(zt_part, both)


def cycle_first(starts, pairs, own, own_c, far, far_c, tail, far_tail, z, zt, swap, *refs):
    units, near_out, away_out = refs[:-2], refs[-2], refs[-1]
    if starts:
        near_out[...], away_out[...] = summed(units, starts, z, zt)
        return
    half_rows = units[0].shape[1] // pairs
    group, _, core, _, half = place()
    spread = spread_counts(tail, far_tail, [swap[p, :1, :1] for p in range(pairs)], half_rows, lanes_of(pairs))
    near_rows, away_rows = rows_of(core, own, own_c, pairs), rows_of(core, far, far_c, pairs)
    first = group - group % half
    near_out[...], away_out[...] = jnp.zeros(near_out.shape, F32), jnp.zeros(away_out.shape, F32)

    def step(k, none):
        part, part_t = mixed_rows(spread, (first + k) ^ (core * half), near_rows, away_rows, pairs, half_rows)
        near_out[...] += dot(units[0][k], part, TN)
        away_out[...] += dot(part_t, units[0][k])
        return none

    lax.fori_loop(0, units[0].shape[0], step, 0)


def cycle_last(n_sends, starts, z, zt, near, away, inverse, inverse_far, bias, base, *refs):
    units, (own_out, *sends), here = refs[: -n_sends - 2], refs[-n_sends - 2 : -1], refs[-1]
    pairs, height, domain = base.shape
    member = lax.axis_index("ints")
    near, away = near[...], away[...]
    if units:
        more, more_away = summed(units, starts, z, zt)
        near, away = near + more, away + more_away
    for p in range(pairs):
        part = slice(p * domain, (p + 1) * domain)
        here[p] = near[:, part] * inverse[p] + (away[part] * inverse_far[p] + bias[p])
    start = pl.ds(pl.multiple_of(member * height, height), height)
    own_out[...] = here[:, start, :] + base[...]
    for offset, send in enumerate(sends, 1):
        to = pl.multiple_of((member ^ offset) * height, height)
        send[...] = here[:, pl.ds(to, height), :].astype(BF16)


VM = pl.BlockSpec(memory_space=pltpu.VMEM)
HB = pl.BlockSpec(memory_space=pltpu.HBM)


def after(value, *others):
    return lax.optimization_barrier((value, *others))[0] if others else value


def stay(value):
    return pltpu.with_memory_space_constraint(value, pltpu.HBM)


def call(kernel, outs, in_specs, name, scratch=(), flops=0):
    return pl.pallas_call(
        kernel,
        out_shape=outs,
        in_specs=in_specs,
        out_specs=jax.tree.map(lambda _: VM, outs),
        scratch_shapes=scratch,
        name=name,
        cost_estimate=pl.CostEstimate(flops=flops, bytes_accessed=0, transcendentals=0) if flops else None,
        compiler_params=pltpu.CompilerParams(vmem_limit_bytes=48 * 1024 * 1024),
    )


def body(
    amps,
    resid_rest,
    int_blocks,
    virt_energy,
    pair_energy,
    item_block,
    share_owner,
    share_pair,
    share_amp,
    transpose_pair,
):
    n_pairs, n_ints = lax.axis_size("pairs"), lax.axis_size("ints")
    pairs, height, domain = amps.shape
    rows, half_rows, half = pairs * height, 2 * height, n_pairs // 2
    shape = jax.ShapeDtypeStruct
    operands = (
        amps,
        int_blocks,
        resid_rest,
        virt_energy,
        pair_energy,
        item_block.reshape(1, -1),
        share_owner.reshape(1, -1),
        share_pair.reshape(1, -1),
        share_amp.reshape(1, -1),
    )
    lean, half_own, tail, resid_half = call(
        prepare,
        [
            shape((rows + TILE, domain), BF16),
            shape((half_rows, domain), BF16),
            shape((TILE + height, domain), BF16),
            shape((rows, domain), BF16),
        ],
        [HB] * len(operands),
        "prepare",
        [(pltpu.SMEM if o is pair_energy else pltpu.VMEM)(o.shape, o.dtype) for o in operands]
        + [pltpu.SemaphoreType.DMA((len(operands),))],
    )(*map(stay, operands))
    inverse, base = call(
        near_factors,
        [shape((pairs, domain, domain), F32), shape((pairs, height, domain), F32)],
        [HB, VM],
        "near_factors",
        [pltpu.VMEM(resid_rest.shape, F32), pltpu.SemaphoreType.DMA],
        10**9,
    )(stay(resid_rest), tail)

    def across(value, *others):
        return exchange(after(value, *others), 0, CORE)

    far, far_tail = exchange(lean, half, 0), exchange(tail, half, 0)
    y_own = [exchange(lean, 0, k) for k in range(2, n_ints, 2)]
    blocks = [family_exchange(half_own, j) for j in range(1, half)] if n_pairs <= DIRECT else []
    y_far = [exchange(after(far, *y_own), 0, k) for k in range(2, n_ints, 2)]
    far_tail_c = across(far_tail)
    if n_pairs <= DIRECT:
        blocks += [across(block) for block in blocks]
    else:
        blocks = [lax.all_gather(half_own, "pairs", axis=0, tiled=False)]
    tall = shape((pairs * domain, half_rows), F32)
    product, ids = call(
        functools.partial(products, len(y_own), item_block.shape[0], pairs),
        [tall, shape(tall.shape, jnp.int32)],
        [VM] * (3 + len(y_own) + len(y_far) + len(blocks)),
        "products",
    )(lean, far, half_own, *y_own, *y_far, *blocks)
    keep, give = call(
        functools.partial(partials, len(y_own), pairs, n_pairs <= DIRECT),
        [shape((pairs * half_rows, domain), BF16)] * 2,
        [VM] * (6 + len(y_own) + len(y_far)),
        "partials",
    )(lean, far, far_tail, far_tail_c, product, ids, *y_own, *y_far)
    inter = call(joined, shape((pairs * half_rows, domain), BF16), [VM] * 2, "joined")(keep, across(give))
    own_c, far_c = across(lean), across(far)
    if n_pairs <= DIRECT:
        units = [inter] + [exchange(inter, j, 0) for j in range(1, half)]
    else:
        every = lax.all_gather(inter, "pairs", axis=0, tiled=False)
        first = lax.axis_index("pairs") // half * half
        units = [lax.dynamic_slice_in_dim(every, first, half, 0)]
    resid_far = exchange(resid_half, half, 0)
    n_units = len(units)
    wide, planned = pairs * half_rows, n_units if n_units > 1 else 0
    z, zt, inverse_far, bias, swap = call(
        functools.partial(factors, planned, pairs),
        [
            shape((n_units * wide, pairs * domain), BF16),
            shape((pairs * domain, n_units * wide), BF16),
            shape((pairs, domain, domain), F32),
            shape((pairs, domain, domain), F32),
            shape((pairs, 8, 128), jnp.int32),
        ],
        [VM] * 7 + [HB],
        "factors",
        [pltpu.SMEM(transpose_pair.shape, jnp.int32), pltpu.SemaphoreType.DMA],
    )(lean, own_c, far, far_c, tail, far_tail, resid_far, stay(transpose_pair))
    early = [0, planned - 1] if planned else []
    late = [k for k in range(planned) if k not in early]
    first_units = [units[k] for k in early] or units
    near, away = call(
        functools.partial(cycle_first, early, pairs),
        [shape((domain, pairs * domain), F32), shape((pairs * domain, domain), F32)],
        [VM] * (9 + len(first_units)),
        "cycle_first",
    )(lean, own_c, far, far_c, tail, far_tail, z, zt, swap, *first_units)
    mine, *sends = call(
        functools.partial(cycle_last, n_ints - 1, late),
        [shape((pairs, height, domain), F32)] + [shape((pairs, height, domain), BF16)] * (n_ints - 1),
        [VM] * (8 + len(late)),
        "cycle_last",
        [pltpu.VMEM((pairs, domain, domain), F32)],
    )(z, zt, near, away, inverse, inverse_far, bias, base, *[units[k] for k in late])
    for offset in [*range(2, n_ints), 1]:
        mine = mine + exchange(sends[offset - 1], 0, offset).astype(F32)
    return -0.5 * mine


def solution(mesh):
    placed = (
        P("pairs", "ints", None),
        P("pairs", "ints", None),
        P("pairs", None, None),
        P("pairs", None),
        P("pairs"),
        P(("pairs", "ints"), None),
        P("pairs", None),
        P("pairs", None),
        P("pairs", None),
        P("pairs"),
    )
    return jax.shard_map(
        body, mesh=mesh, in_specs=placed, out_specs=P("pairs", "ints", None), check_vma=False
    )
```
